256 devices in a mesh: ctx: 32 (over y, z_lo, core), rep: 8 (over z_hi, x).
Axes of the slice: x: 4, y: 4, z: 8 (z_hi: 2, z_lo: 4; z = z_hi * 4 + z_lo), core: 2. Of those that a mesh axis runs over, the one named last changes fastest.
Arguments:
- hidden: bfloat16 [8, 4096, 8192], P('rep', 'ctx'), may hold values from -6 to 6
- queries: bfloat16 [8, 4096, 4096], P('rep', 'ctx'), may hold values from -128 to 128
- keys: bfloat16 [8, 4096, 512], P('rep', 'ctx'), may hold values from -6 to 6
- values: bfloat16 [8, 4096, 512], P('rep', 'ctx'), may hold values from -6 to 6
- out_grad: bfloat16 [8, 4096, 4096], P('rep', 'ctx'), may hold values from -6 to 6
- positions: int32 [8, 4096], P('rep', 'ctx'), may hold values from 0 to 1023, as said below
Outputs:
- query_grad: bfloat16 [8, 4096, 4096], P('rep', 'ctx')
- weight_gradient: float32 [8192, 1024], P('ctx', 'rep')
The draws below stay inside these ranges and needn't reach their ends.
Inputs may be any that keep to these rules, and one draw needn't show every extreme that they name: Within a replica's row each position is 0 (a document starts) or one more than the position before it; the first token's position may exceed 0, its document having begun before the stretch; no document of the stretch spans more than 1024 positions.
All inputs are finite; a program needn't handle non-finite values.
Results may differ from the reference program's by a relative error of at most 0.014.
Values may be sent and summed in bfloat16 or wider, within the bound.
A program may use at most 128 MiB of HBM per device.

```python
import jax
import jax.numpy as jnp
from jax import lax

MODEL_WIDTH = 8192
QUERY_HEADS = 32
KEY_VALUE_HEADS = 4
HEAD_SIZE = 128
LOCAL_TOKENS = 128
STRETCH_TOKENS = 4096
REPLICA_COUNT = 8
DOC_MAX = 1024
N_CTX = 32


def shared_keys(key):
    return jnp.clip(jax.random.normal(key, (REPLICA_COUNT, STRETCH_TOKENS, KEY_VALUE_HEADS * HEAD_SIZE), jnp.float32), -6.0, 6.0)


def draw_keys(key, part):
    start_offset = shared_keys(key)
    return start_offset.astype(jnp.bfloat16)


def draw_queries(key, part):
    key = jax.random.fold_in(key, 23)
    drawn = jnp.clip(jax.random.normal(key, (REPLICA_COUNT, STRETCH_TOKENS, QUERY_HEADS * HEAD_SIZE), jnp.float32), -6.0, 6.0)
    return drawn.astype(jnp.bfloat16)


def draw_positions(key, part):
    key = jax.random.fold_in(key, 37)
    offset_key, extra_key = jax.random.split(key)
    offset = jax.random.randint(offset_key, (REPLICA_COUNT, 1), 0, DOC_MAX)
    index = jnp.arange(STRETCH_TOKENS, dtype=jnp.int32)[None, :]
    forced = (index + offset) % DOC_MAX == 0
    opening = (DOC_MAX - offset) % DOC_MAX
    outside = (index < opening) | (index >= opening + DOC_MAX)
    extra = (jax.random.randint(extra_key, (REPLICA_COUNT, STRETCH_TOKENS), 0, 24) == 0) & outside
    marked = jnp.where(forced | extra, index, -1)
    latest = lax.cummax(marked, axis=1)
    return jnp.where(latest >= 0, index - latest, index + offset).astype(jnp.int32)


def spiked(values, own_key, source, target, blocks, factor):
    def block_of(axis_at):
        return (jnp.arange(values.shape[axis_at]) // (values.shape[axis_at] // blocks)).reshape((-1,) + (1,) * (values.ndim - 1 - axis_at))

    near = jax.random.permutation(own_key, blocks)[block_of(target)]
    far = (block_of(target) + blocks // 2) % blocks
    return jnp.where((block_of(source) == near) | (block_of(source) == far), factor * values, values)


def block_levels(rng, dims, shards, smallest, largest):
    loudness = 1.0
    for position, shards_of in shards:
        heights = jax.random.uniform(jax.random.fold_in(jax.random.fold_in(rng, 6), position), (shards_of,), jnp.float32, smallest / len(shards), largest / len(shards))
        loudness = loudness * jnp.repeat(jnp.exp(heights), dims[position] // shards_of).reshape((-1,) + (1,) * (len(dims) - 1 - position))
    return loudness


def scatter_about(own_key, shape, deviation, most, cuts=(), kind=jnp.bfloat16):
    entries = deviation * jax.random.normal(own_key, shape, jnp.float32)
    if cuts:
        entries = entries * block_levels(own_key, shape, cuts, -0.22, 0.18)
    return jnp.clip(entries, -most, most).astype(kind)


def gaussian_with(key, dims, deviation, limit, cuts, heavy, held_as=jnp.bfloat16):
    entries = deviation * jax.random.normal(key, dims, jnp.float32)
    if cuts:
        entries = entries * block_levels(key, dims, cuts, -0.22, 0.18)
    return jnp.clip(spiked(entries, jax.random.fold_in(key, 3), *heavy), -limit, limit).astype(held_as)


def setup_inputs(seed: int = 0) -> dict:
    key_of = jax.random.split(jax.random.key(seed), 7)
    return {
        "hidden": gaussian_with(key_of[0], (REPLICA_COUNT, STRETCH_TOKENS, MODEL_WIDTH), 1.0, 6.0, ((0, 8), (1, 32)), (1, 2, 32, 2.75)),
        "queries": draw_queries(jax.random.fold_in(key_of[6], 71), 0),
        "keys": draw_keys(jax.random.fold_in(key_of[6], 71), 0),
        "values": scatter_about(key_of[3], (REPLICA_COUNT, STRETCH_TOKENS, KEY_VALUE_HEADS * HEAD_SIZE), 1.0, 6.0, ((0, 8), (1, 32))),
        "out_grad": scatter_about(key_of[4], (REPLICA_COUNT, STRETCH_TOKENS, QUERY_HEADS * HEAD_SIZE), 1.0, 6.0, ((0, 8), (1, 32))),
        "positions": draw_positions(jax.random.fold_in(key_of[6], 71), 0),
    }


def attend_heads(query_heads, grad_heads, key_head_gradient, value_head_gradient, places):
    total = query_heads.shape[0]
    block = min(512, total)
    reach = DOC_MAX
    span = min(total, block + reach)
    scale = HEAD_SIZE ** -0.5

    def one_block(carry, block_index):
        key_acc, value_acc = carry
        first_query = block_index * block
        first_key = jnp.clip(first_query - reach, 0, total - span).astype(jnp.int32)
        query_block = lax.dynamic_slice_in_dim(query_heads, first_query, block, 0).astype(jnp.float32)
        grad_block = lax.dynamic_slice_in_dim(grad_heads, first_query, block, 0).astype(jnp.float32)
        key_window = lax.dynamic_slice_in_dim(key_head_gradient, first_key, span, 0).astype(jnp.float32)
        value_window = lax.dynamic_slice_in_dim(value_head_gradient, first_key, span, 0).astype(jnp.float32)
        place_block = lax.dynamic_slice_in_dim(places, first_query, block, 0)
        scores = jnp.einsum("qhd,khd->hqk", query_block, key_window) * scale
        query_index = first_query + jnp.arange(block, dtype=jnp.int32)
        key_index = first_key + jnp.arange(span, dtype=jnp.int32)
        visible = (key_index[None, :] <= query_index[:, None]) & (key_index[None, :] >= (query_index - place_block)[:, None])
        masked = jnp.where(visible[None], scores, -1e30)
        highest = jnp.max(masked, axis=-1, keepdims=True)
        raised = jnp.where(visible[None], jnp.exp(masked - highest), 0.0)
        probs = raised / jnp.sum(raised, axis=-1, keepdims=True)
        weights = probs.astype(jnp.bfloat16).astype(jnp.float32)
        attended = jnp.einsum("hqk,khd->qhd", weights, value_window)
        delta = jnp.sum(grad_block * attended, axis=-1)
        dprob = jnp.einsum("qhd,khd->hqk", grad_block, value_window)
        dscore = (probs * (dprob - delta.T[:, :, None]) * scale).astype(jnp.bfloat16).astype(jnp.float32)
        query_grad = jnp.einsum("hqk,khd->qhd", dscore, key_window).astype(jnp.bfloat16)
        key_part = jnp.einsum("hqk,qhd->khd", dscore, query_block)
        value_part = jnp.einsum("hqk,qhd->khd", weights, grad_block)
        key_acc = lax.dynamic_update_slice_in_dim(key_acc, lax.dynamic_slice_in_dim(key_acc, first_key, span, 0) + key_part, first_key, 0)
        value_acc = lax.dynamic_update_slice_in_dim(value_acc, lax.dynamic_slice_in_dim(value_acc, first_key, span, 0) + value_part, first_key, 0)
        return (key_acc, value_acc), query_grad

    zero_start = jnp.zeros(key_head_gradient.shape, jnp.float32)
    (key_acc, value_acc), query_grads = lax.scan(one_block, (zero_start, zero_start), jnp.arange(total // block, dtype=jnp.int32))
    return query_grads.reshape(query_heads.shape), key_acc.astype(jnp.bfloat16), value_acc.astype(jnp.bfloat16)


def reference(hidden, queries, keys, values, out_grad, positions):
    group_count = QUERY_HEADS // KEY_VALUE_HEADS

    def one_replica(inputs):
        query_rows, key_row_gradient, value_row_gradient, grad_rows, places = inputs
        query_heads = query_rows.reshape(STRETCH_TOKENS, QUERY_HEADS, HEAD_SIZE)
        grad_heads = grad_rows.reshape(STRETCH_TOKENS, QUERY_HEADS, HEAD_SIZE)
        key_head_gradient = jnp.broadcast_to(key_row_gradient.reshape(STRETCH_TOKENS, KEY_VALUE_HEADS, 1, HEAD_SIZE), (STRETCH_TOKENS, KEY_VALUE_HEADS, group_count, HEAD_SIZE)).reshape(STRETCH_TOKENS, QUERY_HEADS, HEAD_SIZE)
        value_head_gradient = jnp.broadcast_to(value_row_gradient.reshape(STRETCH_TOKENS, KEY_VALUE_HEADS, 1, HEAD_SIZE), (STRETCH_TOKENS, KEY_VALUE_HEADS, group_count, HEAD_SIZE)).reshape(STRETCH_TOKENS, QUERY_HEADS, HEAD_SIZE)
        query_grad, key_per_head, value_per_head = attend_heads(query_heads, grad_heads, key_head_gradient, value_head_gradient, places)
        key_total = key_per_head.astype(jnp.float32).reshape(STRETCH_TOKENS, KEY_VALUE_HEADS, group_count, HEAD_SIZE).sum(axis=2).astype(jnp.bfloat16)
        value_total = value_per_head.astype(jnp.float32).reshape(STRETCH_TOKENS, KEY_VALUE_HEADS, group_count, HEAD_SIZE).sum(axis=2).astype(jnp.bfloat16)
        key_value_gradients = jnp.concatenate([key_total.reshape(STRETCH_TOKENS, KEY_VALUE_HEADS * HEAD_SIZE), value_total.reshape(STRETCH_TOKENS, KEY_VALUE_HEADS * HEAD_SIZE)], axis=1)
        return query_grad.reshape(STRETCH_TOKENS, QUERY_HEADS * HEAD_SIZE), key_value_gradients

    query_grad, key_value_gradients = lax.map(one_replica, (queries, keys, values, out_grad, positions))
    hidden_sequences = hidden.reshape(REPLICA_COUNT * N_CTX, LOCAL_TOKENS, MODEL_WIDTH)
    gradient_runs = key_value_gradients.reshape(REPLICA_COUNT * N_CTX, LOCAL_TOKENS, 2 * KEY_VALUE_HEADS * HEAD_SIZE)

    def accumulate_term(total, pair):
        term = jnp.dot(pair[0].T, pair[1], preferred_element_type=jnp.float32)
        rounded = lax.optimization_barrier(term.astype(jnp.bfloat16))
        return total + rounded.astype(jnp.float32), None

    weight_gradient, unused_slot = lax.scan(accumulate_term, jnp.zeros((MODEL_WIDTH, 2 * KEY_VALUE_HEADS * HEAD_SIZE), jnp.float32), (hidden_sequences, gradient_runs))
    return query_grad, weight_gradient
```

```python
import functools
import math

import jax
import jax.numpy as jnp
from jax import lax
from jax.experimental import pallas as pl
from jax.experimental.pallas import tpu as pltpu
from jax.sharding import PartitionSpec as P

GROUPS = 4
SHARE = 8
D = 128
L = 128
NY, NZL, NZH, NX = 4, 4, 2, 4
HC = 4
ROWS = 256
TILE = 4

F32, BF16 = jnp.float32, jnp.bfloat16
NT = (((1,), (1,)), ((), ()))
TN = (((0,), (0,)), ((), ()))
NN = (((1,), (0,)), ((), ()))


def dot(a, b, dims):
    return lax.dot_general(a, b, dims, preferred_element_type=F32)


def kernel(
    hidden, queries, keys, values, out_grad, positions, dq_out, w_out,
    q_s, go_s, kv, bias, t_s, dp_s, w_s, ds_s, acc, dq_s,
    pair_send, pair_recv, back_send, back_recv, own_s, grads, hid, w_send, w_recv, e_send, e_recv, f_send, f_recv,
    in_sem, dq_sem, a_send, a_recv, af_send, af_recv, h_send, h_recv, h_loc,
    p_ss, p_rs, b_ss, b_rs, g_ss, g_rs, gf_ss, gf_rs, w_ss, w_rs, e_ss, e_rs, f_ss, f_rs,
):
    nctx = NY * NZL * 2
    nz = NZL * NZH
    nb = 2 * HC + 1
    m = NZL * ROWS
    part = D // NY
    tiles = SHARE // TILE
    lanes = TILE * L
    scale = D ** -0.5

    i = lax.axis_index("ctx")
    r = lax.axis_index("rep")
    c = i % 2
    z_lo = (i // 2) % NZL
    y = i // (2 * NZL)
    x = r % NX
    z_hi = r // NX
    zz = z_hi * NZL + z_lo
    sib = i + 1 - 2 * c

    def at(ctx, rep):
        return {"ctx": ctx, "rep": rep}

    def ctx_of(yy, zl, cc):
        return (yy * NZL + zl) * 2 + cc

    def around(d):
        return (i + 2 * d + nctx) % nctx

    def rep_at(d):
        return z_hi * NX + (x + d) % NX

    def y_at(d):
        return (y + d) % NY

    def z_at(d):
        other = (zz + d) % nz
        return other, at(ctx_of(y, other % NZL, c), (other // NZL) * NX + x)

    q_in = pltpu.make_async_copy(queries.at[0], q_s, in_sem.at[0])
    go_in = pltpu.make_async_copy(out_grad.at[0], go_s, in_sem.at[1])
    q_in.start()
    go_in.start()

    barrier = pltpu.get_barrier_semaphore()
    partners = [at(sib, r)]
    for k in range(1, HC + 1):
        partners += [at(around(k), r), at(around(-k), r)]
    for d in range(1, NX):
        partners += [at(i, rep_at(d)), at(sib, rep_at(d))]
    for d in range(1, NY):
        partners.append(at(ctx_of(y_at(d), z_lo, c), r))
    for d in range(1, nz):
        partners.append(z_at(d)[1])
    for partner in partners:
        pl.semaphore_signal(barrier, inc=1, device_id=partner, device_id_type=pl.DeviceIdType.MESH)

    def final_target(g):
        return at(ctx_of(x, z_lo, c), z_hi * NX + g)

    def final_source(q):
        return at(ctx_of(q, z_lo, c), z_hi * NX + y)

    on_diagonal = x == y
    for g in range(NX):
        away = jnp.logical_not(jnp.logical_and(on_diagonal, g == x))

        @pl.when(away)
        def _():
            pl.semaphore_signal(barrier, inc=1, device_id=final_target(g), device_id_type=pl.DeviceIdType.MESH)
            pl.semaphore_signal(barrier, inc=1, device_id=final_source(g), device_id_type=pl.DeviceIdType.MESH)

    for g in range(GROUPS):
        kv[g, HC, c, :, 0:D] = keys[0, :, g * D:(g + 1) * D]
        kv[g, HC, c, :, D:2 * D] = values[0, :, g * D:(g + 1) * D]

    count = len(partners) + 2 * NX - 2 * jnp.where(on_diagonal, 1, 0)
    pl.semaphore_wait(barrier, count)

    def remote(src, dst, send, recv, where):
        return pltpu.make_async_remote_copy(
            src_ref=src, dst_ref=dst, send_sem=send, recv_sem=recv, device_id=where, device_id_type=pl.DeviceIdType.MESH
        )

    def halo(g, k):
        return remote(kv.at[g, HC, c], kv.at[g, HC - k, c], a_send.at[g, k - 1], a_recv.at[g, k - 1], at(around(k), r))

    def pair_kv(g):
        blocks = pl.ds(1 - c, HC)
        return remote(kv.at[g, blocks, c], kv.at[g, blocks, c], af_send.at[g], af_recv.at[g], at(sib, r))

    def pair_kv_in(g):
        blocks = pl.ds(c, HC)
        return remote(kv.at[g, blocks, 1 - c], kv.at[g, blocks, 1 - c], af_send.at[g], af_recv.at[g], at(sib, r))

    for g in range(GROUPS):
        for k in range(1, HC + 1):
            halo(g, k).start()

    def hidden_copy(dx, dc, zl):
        xx = (x + dx) % NX
        cc = (c + dc) % 2
        src = hidden.at[0, :, pl.ds(pl.multiple_of(((xx * NZL + zl) * 2 + cc) * ROWS, ROWS), ROWS)]
        dst = hid.at[2 * x + c, :, pl.ds(zl * ROWS, ROWS)]
        slot = 2 * dx + dc
        if slot == 0:
            return pltpu.make_async_copy(src, dst, h_loc.at[zl])
        return remote(src, dst, h_send.at[slot, zl], h_recv.at[slot, zl], at(ctx_of(y, z_lo, cc), rep_at(dx)))

    for dx in range(NX):
        for dc in range(2):
            for zl in range(NZL):
                hidden_copy(dx, dc, zl).start()

    token = lax.broadcasted_iota(jnp.int32, (L, L), 1) + i * L
    lowest = jnp.maximum(token - jnp.broadcast_to(positions[...], (L, L)), 0)
    for kc in range(nb):
        key = lax.broadcasted_iota(jnp.int32, (L, L), 0) + (i - 2 * HC + kc) * L
        seen = jnp.logical_and(key <= token, key >= lowest)
        bias[kc] = jnp.where(seen, 0.0, -1e30)

    q_in.wait()
    go_in.wait()

    def get_pair_kv(g):
        for k in range(1, HC + 1):
            halo(g, k).wait_recv()
        pair_kv(g).start()

    get_pair_kv(0)

    def attend(t):
        g = t // tiles
        cols = pl.ds(pl.multiple_of(t * lanes, lanes), lanes)
        q_wide = q_s[:, cols]
        go_wide = go_s[:, cols]
        q2 = jnp.concatenate([q_wide[:, j * D:(j + 1) * D] for j in range(TILE)], axis=0)
        go2 = jnp.concatenate([go_wide[:, j * D:(j + 1) * D] for j in range(TILE)], axis=0)

        def block(kc):
            b = c + kc
            return kv[g, b // 2, b % 2]

        def fold(v):
            return v.reshape(L // 8, 8, lanes)

        top = None
        for kc in range(nb):
            s = dot(block(kc)[:, 0:D], q2, NT) + jnp.concatenate([bias[kc]] * TILE, axis=1)
            t_s[kc] = s
            high = jnp.max(fold(s), axis=0)
            top = high if top is None else jnp.maximum(top, high)
        top = jnp.max(top, axis=0, keepdims=True)
        total = jnp.zeros((8, lanes), F32)
        delta = jnp.zeros((8, lanes), F32)
        for kc in range(nb):
            p = jnp.exp2((t_s[kc] - top) * (scale * math.log2(math.e)))
            dp = dot(block(kc)[:, D:2 * D], go2, NT)
            t_s[kc] = p
            dp_s[kc] = dp
            total += jnp.sum(fold(p), axis=0)
            delta += jnp.sum(fold(p * dp), axis=0)
        inverse = 1.0 / jnp.sum(total, axis=0, keepdims=True)
        delta = jnp.sum(delta, axis=0, keepdims=True) * inverse
        for kc in range(nb):
            p = t_s[kc] * inverse
            w_s[kc] = p.astype(BF16)
            ds_s[kc] = (p * (dp_s[kc] - delta)).astype(BF16)
        dq = jnp.zeros((lanes, D), F32)
        for kc in range(nb):
            b = c + kc
            ds = ds_s[kc]
            acc[g % 2, b % 2, b // 2, :, 0:D] += dot(ds, q2, NN)
            acc[g % 2, b % 2, b // 2, :, D:2 * D] += dot(w_s[kc], go2, NN)
            dq += dot(ds, block(kc)[:, 0:D], TN)
        dq = (dq * scale).astype(BF16)
        dq_s[t] = jnp.concatenate([dq[j * L:(j + 1) * L] for j in range(TILE)], axis=1)
        dq_copy(t).start()

    def dq_copy(t):
        cols = pl.ds(pl.multiple_of(t * lanes, lanes), lanes)
        return pltpu.make_async_copy(dq_s.at[t], dq_out.at[0, :, cols], dq_sem.at[t])

    def pair_grads(g):
        return remote(pair_send.at[g, pl.ds(c, HC)], pair_recv.at[g, pl.ds(c, HC)], p_ss.at[g], p_rs.at[g], at(sib, r))

    def pair_grads_in(g):
        blocks = pl.ds(1 - c, HC)
        return remote(pair_send.at[g, blocks], pair_recv.at[g, blocks], p_ss.at[g], p_rs.at[g], at(sib, r))

    def stage0(g):
        pair_send[g] = acc[g % 2, 1 - c].astype(BF16)
        pair_recv[g, HC * c] = jnp.zeros((L, 2 * D), BF16)
        pair_grads(g).start()

    def back(g, k):
        return remote(back_send.at[g, k], back_recv.at[g, k], b_ss.at[g, k], b_rs.at[g, k], at(around(k - HC), r))

    def stage1(g):
        pair_grads_in(g).wait_recv()
        for k in range(HC):
            back_send[g, k] = (acc[g % 2, c, k] + pair_recv[g, k].astype(F32)).astype(BF16)
            back(g, k).start()
        own_s[...] = acc[g % 2, c, HC] + pair_recv[g, HC].astype(F32)

    def spread(g, d):
        mine = grads.at[g, x, c]
        return remote(mine, mine, g_ss.at[g, d - 1], g_rs.at[g, d - 1], at(i, rep_at(d)))

    def stage2(g):
        whole = own_s[...]
        for k in range(HC):
            back(g, k).wait_recv()
            whole += back_recv[g, k].astype(F32)
        grads[g, x, c, :, 0:D] = (whole[:, 0:D] * scale).astype(BF16)
        grads[g, x, c, :, D:2 * D] = whole[:, D:2 * D].astype(BF16)
        for d in range(1, NX):
            spread(g, d).start()

    def pair_spread(g, cc):
        half = grads.at[g, :, cc]
        return remote(half, half, gf_ss.at[g], gf_rs.at[g], at(sib, r))

    def stage3(g):
        for d in range(1, NX):
            spread(g, d).wait_recv()
        pair_spread(g, c).start()

    def w_copy(g, d):
        return remote(w_send.at[g, y_at(d)], w_recv.at[g, d - 1], w_ss.at[g, d - 1], w_rs.at[g, d - 1],
                      at(ctx_of(y_at(d), z_lo, c), r))

    def stage4(g):
        @pl.when(g == 0)
        def _():
            for dx in range(NX):
                for dc in range(2):
                    for zl in range(NZL):
                        copy = hidden_copy(dx, dc, zl)
                        copy.wait() if dx + dc == 0 else copy.wait_recv()

        pair_spread(g, 1 - c).wait_recv()
        tokens = NX * 2 * L
        got = dot(grads[g].reshape(tokens, 2 * D), hid[...].reshape(tokens, m), TN).astype(BF16)
        for j in range(NY):
            w_send[g, j, 0:part] = got[j * part:(j + 1) * part]
            w_send[g, j, part:2 * part] = got[D + j * part:D + (j + 1) * part]
        for d in range(1, NY):
            w_copy(g, d).start()

    def e_copy(g, d):
        other, where = z_at(d)
        return remote(e_send.at[g, other], e_recv.at[g, d - 1], e_ss.at[g, d - 1], e_rs.at[g, d - 1], where)

    def stage5(g):
        whole = w_send[g, y].astype(F32)
        for d in range(1, NY):
            w_copy(g, d).wait_recv()
            whole += w_recv[g, d - 1].astype(F32)
        for zh in range(NZH):
            for zl in range(NZL):
                e_send[g, zh * NZL + zl] = whole[zh * part:(zh + 1) * part, zl * ROWS:(zl + 1) * ROWS].astype(BF16)
        for d in range(1, nz):
            e_copy(g, d).start()

    def f_copy(g):
        return remote(f_send.at[g], f_recv.at[y], f_ss.at[g], f_rs.at[y], final_target(g))

    def stays(g):
        return jnp.logical_and(on_diagonal, g == x)

    def stage6(g):
        whole = e_send[g, zz].astype(F32)
        for d in range(1, nz):
            e_copy(g, d).wait_recv()
            whole += e_recv[g, d - 1].astype(F32)

        @pl.when(stays(g))
        def _():
            f_recv[y] = whole

        @pl.when(jnp.logical_not(stays(g)))
        def _():
            f_send[g] = whole
            f_copy(g).start()

    stages = (stage0, stage1, stage2, stage3, stage4, stage5, stage6)

    def step(t, nothing):
        @pl.when(t < GROUPS * tiles)
        def _():
            g = t // tiles

            @pl.when(t % tiles == 0)
            def _():
                acc[g % 2] = jnp.zeros((2, HC + 1, L, 2 * D), F32)
                pair_kv_in(g).wait_recv()

                @pl.when(g + 1 < GROUPS)
                def _():
                    get_pair_kv(g + 1)

            attend(t)

        for s, stage in enumerate(stages):
            since = t - s - (tiles - 1)

            @pl.when(jnp.logical_and(since % tiles == 0, jnp.logical_and(since >= 0, since < GROUPS * tiles)))
            def _():
                stage(since // tiles)

        return nothing

    lax.fori_loop(0, (GROUPS - 1) * tiles + tiles - 1 + len(stages), step, 0)

    for q in range(NY):
        here = jnp.logical_and(on_diagonal, q == y)

        @pl.when(jnp.logical_not(here))
        def _():
            remote(f_send.at[0], f_recv.at[q], f_ss.at[0], f_rs.at[q], final_source(q)).wait_recv()

    w_out[...] = jnp.transpose(f_recv[...].reshape(D, ROWS))

    for t in range(GROUPS * tiles):
        dq_copy(t).wait()
    for g in range(GROUPS):
        for k in range(1, HC + 1):
            halo(g, k).wait_send()
        pair_kv(g).wait_send()
        pair_grads(g).wait_send()
        for k in range(HC):
            back(g, k).wait_send()
        for d in range(1, NX):
            spread(g, d).wait_send()
        pair_spread(g, c).wait_send()
        for d in range(1, NY):
            w_copy(g, d).wait_send()
        for d in range(1, nz):
            e_copy(g, d).wait_send()

        @pl.when(jnp.logical_not(stays(g)))
        def _():
            f_copy(g).wait_send()

    for dx in range(NX):
        for dc in range(2):
            for zl in range(NZL):
                if dx + dc:
                    hidden_copy(dx, dc, zl).wait_send()


def body(hidden, queries, keys, values, out_grad, positions):
    nb, nz, m, part = 2 * HC + 1, NZL * NZH, NZL * ROWS, D // NY
    tiles, lanes = SHARE // TILE, TILE * L
    vmem, dma = pltpu.VMEM, pltpu.SemaphoreType.DMA
    anywhere, inside = pl.BlockSpec(memory_space=pl.ANY), pl.BlockSpec(memory_space=pltpu.VMEM)
    pairs = GROUPS * SHARE * L * L * nb
    return pl.pallas_call(
        kernel,
        out_shape=(
            jax.ShapeDtypeStruct(queries.shape, BF16),
            jax.ShapeDtypeStruct((ROWS, D), F32),
        ),
        in_specs=[anywhere, anywhere, inside, inside, anywhere, inside],
        out_specs=(anywhere, inside),
        scratch_shapes=[
            vmem(queries.shape[1:], BF16),
            vmem(queries.shape[1:], BF16),
            vmem((GROUPS, HC + 1, 2, L, 2 * D), BF16),
            vmem((nb, L, L), F32),
            vmem((nb, L, lanes), F32),
            vmem((nb, L, lanes), F32),
            vmem((nb, L, lanes), BF16),
            vmem((nb, L, lanes), BF16),
            vmem((2, 2, HC + 1, L, 2 * D), F32),
            vmem((GROUPS * tiles, L, lanes), BF16),
            vmem((GROUPS, HC + 1, L, 2 * D), BF16),
            vmem((GROUPS, HC + 1, L, 2 * D), BF16),
            vmem((GROUPS, HC, L, 2 * D), BF16),
            vmem((GROUPS, HC, L, 2 * D), BF16),
            vmem((L, 2 * D), F32),
            vmem((GROUPS, NX, 2, L, 2 * D), BF16),
            vmem((NX * 2, L, m), BF16),
            vmem((GROUPS, NY, 2 * part, m), BF16),
            vmem((GROUPS, NY - 1, 2 * part, m), BF16),
            vmem((GROUPS, nz, part, ROWS), BF16),
            vmem((GROUPS, nz - 1, part, ROWS), BF16),
            vmem((GROUPS, part, ROWS), F32),
            vmem((NY, part, ROWS), F32),
            dma((2,)),
            dma((GROUPS * tiles,)),
            dma((GROUPS, HC)), dma((GROUPS, HC)),
            dma((GROUPS,)), dma((GROUPS,)),
            dma((2 * NX, NZL)), dma((2 * NX, NZL)), dma((NZL,)),
            dma((GROUPS,)), dma((GROUPS,)),
            dma((GROUPS, HC)), dma((GROUPS, HC)),
            dma((GROUPS, NX - 1)), dma((GROUPS, NX - 1)),
            dma((GROUPS,)), dma((GROUPS,)),
            dma((GROUPS, NY - 1)), dma((GROUPS, NY - 1)),
            dma((GROUPS, nz - 1)), dma((GROUPS, nz - 1)),
            dma((GROUPS,)), dma((NY,)),
        ],
        compiler_params=pltpu.CompilerParams(
            collective_id=0, has_side_effects=True, vmem_limit_bytes=56 * 2**20
        ),
        cost_estimate=pl.CostEstimate(
            flops=10 * pairs * D, bytes_accessed=12 * 2**20, transcendentals=pairs
        ),
    )(hidden, queries, keys, values, out_grad, positions)


def solution(mesh):
    rows = P("rep", "ctx", None)
    return jax.shard_map(
        body,
        mesh=mesh,
        in_specs=(rows, rows, rows, rows, rows, P("rep", "ctx")),
        out_specs=(rows, P("ctx", "rep")),
        check_vma=False,
    )
```

```python
import functools
import math

import jax
import jax.numpy as jnp
from jax import lax
from jax.experimental import pallas as pl
from jax.experimental.pallas import tpu as pltpu
from jax.sharding import PartitionSpec as P

GROUPS = 4
SHARE = 8
D = 128
L = 128
NY, NZL, NZH, NX = 4, 4, 2, 4
HC = 4
ROWS = 256
TILE = 4
WHEN = ((1, 2), (2, 2), (4, 2), (7, 1), (8, 1), (8, 1), (10, 1), (11, 1))

F32, BF16 = jnp.float32, jnp.bfloat16
NT = (((1,), (1,)), ((), ()))
TN = (((0,), (0,)), ((), ()))
NN = (((1,), (0,)), ((), ()))


def dot(a, b, dims):
    return lax.dot_general(a, b, dims, preferred_element_type=F32)


def kernel(
    hidden, queries, keys, values, out_grad, positions, dq_out, w_out,
    q_s, go_s, kv, bias, t_s, dp_s, w_s, ds_s, acc, dq_s,
    pair_send, pair_recv, back_send, back_recv, relay_recv, own_s, grads, hid, w_send, w_recv, e_send, e_recv, f_send, f_recv,
    in_sem, dq_sem, a_send, a_recv, fw_send, af_send, af_recv, h_send, h_recv, h_loc,
    p_ss, p_rs, r_ss, r_rs, b_ss, b_rs, g_ss, g_rs, gf_ss, gf_rs, w_ss, w_rs, e_ss, e_rs, f_ss, f_rs,
):
    nctx = NY * NZL * 2
    nz = NZL * NZH
    nb = 2 * HC + 1
    m = NZL * ROWS
    part = D // NY
    tiles = SHARE // TILE
    lanes = TILE * L
    scale = D ** -0.5

    i = lax.axis_index("ctx")
    r = lax.axis_index("rep")
    c = i % 2
    z_lo = (i // 2) % NZL
    y = i // (2 * NZL)
    x = r % NX
    z_hi = r // NX
    zz = z_hi * NZL + z_lo
    sib = i + 1 - 2 * c

    def at(ctx, rep):
        return {"ctx": ctx, "rep": rep}

    def ctx_of(yy, zl, cc):
        return (yy * NZL + zl) * 2 + cc

    def around(d):
        return (i + 2 * d + nctx) % nctx

    def rep_at(d):
        return z_hi * NX + (x + d) % NX

    def y_at(d):
        return (y + d) % NY

    def z_at(d):
        other = (zz + d) % nz
        return other, at(ctx_of(y, other % NZL, c), (other // NZL) * NX + x)

    q_in = pltpu.make_async_copy(queries.at[0], q_s, in_sem.at[0])
    go_in = pltpu.make_async_copy(out_grad.at[0], go_s, in_sem.at[1])
    q_in.start()
    go_in.start()

    barrier = pltpu.get_barrier_semaphore()
    partners = [at(sib, r)]
    for k in range(1, HC + 1):
        partners += [at(around(k), r), at(around(-k), r)]
    for d in range(1, NX):
        partners += [at(i, rep_at(d)), at(sib, rep_at(d))]
    for d in range(1, NY):
        partners.append(at(ctx_of(y_at(d), z_lo, c), r))
    for d in range(1, nz):
        partners.append(z_at(d)[1])
    for partner in partners:
        pl.semaphore_signal(barrier, inc=1, device_id=partner, device_id_type=pl.DeviceIdType.MESH)

    def final_target(g):
        return at(ctx_of(x, z_lo, c), z_hi * NX + g)

    def final_source(q):
        return at(ctx_of(q, z_lo, c), z_hi * NX + y)

    on_diagonal = x == y
    for g in range(NX):
        away = jnp.logical_not(jnp.logical_and(on_diagonal, g == x))

        @pl.when(away)
        def _():
            pl.semaphore_signal(barrier, inc=1, device_id=final_target(g), device_id_type=pl.DeviceIdType.MESH)
            pl.semaphore_signal(barrier, inc=1, device_id=final_source(g), device_id_type=pl.DeviceIdType.MESH)

    for g in range(GROUPS):
        kv[g, HC, c, :, 0:D] = keys[0, :, g * D:(g + 1) * D]
        kv[g, HC, c, :, D:2 * D] = values[0, :, g * D:(g + 1) * D]

    count = len(partners) + 2 * NX - 2 * jnp.where(on_diagonal, 1, 0)
    pl.semaphore_wait(barrier, count)

    def remote(src, dst, send, recv, where):
        return pltpu.make_async_remote_copy(
            src_ref=src, dst_ref=dst, send_sem=send, recv_sem=recv, device_id=where, device_id_type=pl.DeviceIdType.MESH
        )

    def halo(g, k):
        return remote(kv.at[g, HC, c], kv.at[g, HC - k, c], a_send.at[g, k - 1], a_recv.at[g, k - 1], at(around(k), r))

    def pair_kv(g):
        blocks = pl.ds(1 - c, HC)
        return remote(kv.at[g, blocks, c], kv.at[g, blocks, c], af_send.at[g], af_recv.at[g], at(sib, r))

    def pair_kv_in(g):
        blocks = pl.ds(c, HC)
        return remote(kv.at[g, blocks, 1 - c], kv.at[g, blocks, 1 - c], af_send.at[g], af_recv.at[g], at(sib, r))

    def direct(k):
        there = z_lo + k
        along = jnp.logical_and(there < NZL, jnp.logical_or(there < NZL - 1, k == 1))
        down = jnp.logical_and(there >= NZL, jnp.logical_or((there - NZL) % NZL > 0, k == HC))
        return jnp.logical_or(along, down)

    def to_last(g, k):
        there = at(around(1), r)
        return remote(kv.at[g, HC - k, c], kv.at[g, HC - k - 1, c], fw_send.at[g, k - 1], a_recv.at[g, k], there)

    def to_first(g, k):
        there = at(around(-1), r)
        return remote(kv.at[g, HC - k, c], kv.at[g, HC - k + 1, c], fw_send.at[g, k - 1], a_recv.at[g, k - 2], there)

    passes_last = jnp.logical_and(z_lo == NZL - 2, NZL > 2)
    passes_first = z_lo == 1
    last_by = range(1, NZL - 1)
    first_by = range(2, HC + 1)

    def send_kv(g):
        for k in range(1, HC + 1):

            @pl.when(jnp.logical_or(g == 0, direct(k)))
            def _():
                halo(g, k).start()

    def kv_sent(g):
        for k in range(1, HC + 1):

            @pl.when(jnp.logical_or(g == 0, direct(k)))
            def _():
                halo(g, k).wait_send()

    send_kv(0)

    def hidden_copy(dx, dc, zl):
        xx = (x + dx) % NX
        cc = (c + dc) % 2
        src = hidden.at[0, :, pl.ds(pl.multiple_of(((xx * NZL + zl) * 2 + cc) * ROWS, ROWS), ROWS)]
        dst = hid.at[2 * x + c, :, pl.ds(zl * ROWS, ROWS)]
        slot = 2 * dx + dc
        if slot == 0:
            return pltpu.make_async_copy(src, dst, h_loc.at[zl])
        return remote(src, dst, h_send.at[slot, zl], h_recv.at[slot, zl], at(ctx_of(y, z_lo, cc), rep_at(dx)))

    for dx in range(NX):
        for dc in range(2):
            for zl in range(NZL):
                hidden_copy(dx, dc, zl).start()

    token = lax.broadcasted_iota(jnp.int32, (L, L), 1) + i * L
    lowest = jnp.maximum(token - jnp.broadcast_to(positions[...], (L, L)), 0)
    for kc in range(nb):
        key = lax.broadcasted_iota(jnp.int32, (L, L), 0) + (i - 2 * HC + kc) * L
        seen = jnp.logical_and(key <= token, key >= lowest)
        bias[kc] = jnp.where(seen, 0.0, -1e30)

    q_in.wait()
    go_in.wait()


    def passes(k):
        return jnp.logical_or(
            jnp.logical_and(passes_last, k in last_by), jnp.logical_and(passes_first, k in first_by)
        )

    def pass_on(g):
        @pl.when(passes_last)
        def _():
            for k in last_by:
                halo(g, k).wait_recv()
                to_last(g, k).start()

        @pl.when(passes_first)
        def _():
            for k in reversed(first_by):
                halo(g, k).wait_recv()
                to_first(g, k).start()

    def to_pair(g):
        for k in range(1, HC + 1):

            @pl.when(jnp.logical_or(g == 0, jnp.logical_not(passes(k))))
            def _():
                halo(g, k).wait_recv()

        pair_kv(g).start()

    kv_sent(0)
    send_kv(1)
    to_pair(0)

    def attend(t):
        g = t // tiles
        cols = pl.ds(pl.multiple_of(t * lanes, lanes), lanes)
        q_wide = q_s[:, cols]
        go_wide = go_s[:, cols]
        q2 = jnp.concatenate([q_wide[:, j * D:(j + 1) * D] for j in range(TILE)], axis=0)
        go2 = jnp.concatenate([go_wide[:, j * D:(j + 1) * D] for j in range(TILE)], axis=0)

        def block(kc):
            b = c + kc
            return kv[g, b // 2, b % 2]

        def fold(v):
            return v.reshape(L // 8, 8, lanes)

        top = None
        for kc in range(nb):
            s = dot(block(kc)[:, 0:D], q2, NT) + jnp.concatenate([bias[kc]] * TILE, axis=1)
            t_s[kc] = s
            high = jnp.max(fold(s), axis=0)
            top = high if top is None else jnp.maximum(top, high)
        top = jnp.max(top, axis=0, keepdims=True)
        total = jnp.zeros((8, lanes), F32)
        delta = jnp.zeros((8, lanes), F32)
        for kc in range(nb):
            p = jnp.exp2((t_s[kc] - top) * (scale * math.log2(math.e)))
            dp = dot(block(kc)[:, D:2 * D], go2, NT)
            t_s[kc] = p
            dp_s[kc] = dp
            total += jnp.sum(fold(p), axis=0)
            delta += jnp.sum(fold(p * dp), axis=0)
        inverse = 1.0 / jnp.sum(total, axis=0, keepdims=True)
        delta = jnp.sum(delta, axis=0, keepdims=True) * inverse
        for kc in range(nb):
            p = t_s[kc] * inverse
            w_s[kc] = p.astype(BF16)
            ds_s[kc] = (p * (dp_s[kc] - delta)).astype(BF16)
        dq = jnp.zeros((lanes, D), F32)
        for kc in range(nb):
            b = c + kc
            ds = ds_s[kc]
            acc[g % 2, b % 2, b // 2, :, 0:D] += dot(ds, q2, NN)
            acc[g % 2, b % 2, b // 2, :, D:2 * D] += dot(w_s[kc], go2, NN)
            dq += dot(ds, block(kc)[:, 0:D], TN)
        dq = (dq * scale).astype(BF16)
        dq_s[t] = jnp.concatenate([dq[j * L:(j + 1) * L] for j in range(TILE)], axis=1)
        dq_copy(t).start()

    def dq_copy(t):
        cols = pl.ds(pl.multiple_of(t * lanes, lanes), lanes)
        return pltpu.make_async_copy(dq_s.at[t], dq_out.at[0, :, cols], dq_sem.at[t])

    def pair_grads(g):
        return remote(pair_send.at[g, pl.ds(c, HC)], pair_recv.at[g, pl.ds(c, HC)], p_ss.at[g], p_rs.at[g], at(sib, r))

    def pair_grads_in(g):
        blocks = pl.ds(1 - c, HC)
        return remote(pair_send.at[g, blocks], pair_recv.at[g, blocks], p_ss.at[g], p_rs.at[g], at(sib, r))

    def stage0(g):
        pair_send[g] = acc[g % 2, 1 - c].astype(BF16)
        pair_recv[g, HC * c] = jnp.zeros((L, 2 * D), BF16)
        pair_grads(g).start()

    def back(g, k):
        return remote(back_send.at[g, k], back_recv.at[g, k], b_ss.at[g, k], b_rs.at[g, k], at(around(k - HC), r))

    def comes_direct(k):
        along = jnp.logical_and(k <= z_lo, jnp.logical_or(z_lo < NZL - 1, k == 1))
        down = jnp.logical_and(k > z_lo, jnp.logical_or(z_lo > 0, k == HC))
        return jnp.logical_or(along, down)

    def relayed(g):
        return g < GROUPS - 1

    def relay_down(g, k):
        return remote(back_send.at[g, HC - k], relay_recv.at[g, k - 2], r_ss.at[g, k - 1], r_rs.at[g, k - 2], at(around(-1), r))

    def relay_up(g, k):
        return remote(back_send.at[g, HC - k], relay_recv.at[g, k - 1], r_ss.at[g, k - 1], r_rs.at[g, k - 1], at(around(1), r))

    def relay_roles(g, k):
        by = jnp.logical_and(relayed(g), jnp.logical_not(comes_direct(k)))
        holds = jnp.logical_and(relayed(g), passes(k))
        return by, holds, jnp.logical_not(jnp.logical_or(by, holds))

    def stage1(g):
        pair_grads_in(g).wait_recv()
        for k in range(1, HC + 1):
            n = HC - k
            back_send[g, n] = (acc[g % 2, c, n] + pair_recv[g, n].astype(F32)).astype(BF16)
            by, holds, plain = relay_roles(g, k)

            @pl.when(plain)
            def _():
                back(g, n).start()

            if k >= 2:

                @pl.when(jnp.logical_and(by, z_lo == NZL - 1))
                def _():
                    relay_down(g, k).start()

            if k < HC:

                @pl.when(jnp.logical_and(by, z_lo == 0))
                def _():
                    relay_up(g, k).start()

        own_s[g] = acc[g % 2, c, HC] + pair_recv[g, HC].astype(F32)

    def stage1b(g):
        def add_and_send(k, copy, slot):
            copy.wait_recv()
            n = HC - k
            back_send[g, n] = (back_send[g, n].astype(F32) + relay_recv[g, slot].astype(F32)).astype(BF16)
            back(g, n).start()

        @pl.when(jnp.logical_and(relayed(g), passes_last))
        def _():
            for k in last_by:
                add_and_send(k, relay_down(g, k + 1), k - 1)

        @pl.when(jnp.logical_and(relayed(g), passes_first))
        def _():
            for k in first_by:
                add_and_send(k, relay_up(g, k - 1), k - 2)

    def spread(g, d):
        mine = grads.at[g, x, c]
        return remote(mine, mine, g_ss.at[g, d - 1], g_rs.at[g, d - 1], at(i, rep_at(d)))

    def stage2(g):
        for k in range(1, HC + 1):

            @pl.when(jnp.logical_or(jnp.logical_not(relayed(g)), direct(k)))
            def _():
                back(g, HC - k).wait_recv()
                own_s[g] += back_recv[g, HC - k].astype(F32)

        whole = own_s[g]
        grads[g, x, c, :, 0:D] = (whole[:, 0:D] * scale).astype(BF16)
        grads[g, x, c, :, D:2 * D] = whole[:, D:2 * D].astype(BF16)
        for d in range(1, NX):
            spread(g, d).start()

    def pair_spread(g, cc):
        half = grads.at[g, :, cc]
        return remote(half, half, gf_ss.at[g], gf_rs.at[g], at(sib, r))

    def stage3(g):
        for d in range(1, NX):
            spread(g, d).wait_recv()
        pair_spread(g, c).start()

    def w_copy(g, d):
        return remote(w_send.at[g, y_at(d)], w_recv.at[g, d - 1], w_ss.at[g, d - 1], w_rs.at[g, d - 1],
                      at(ctx_of(y_at(d), z_lo, c), r))

    def stage4(g):
        @pl.when(g == 0)
        def _():
            for dx in range(NX):
                for dc in range(2):
                    for zl in range(NZL):
                        copy = hidden_copy(dx, dc, zl)
                        copy.wait() if dx + dc == 0 else copy.wait_recv()

        pair_spread(g, 1 - c).wait_recv()
        tokens = NX * 2 * L
        got = dot(grads[g].reshape(tokens, 2 * D), hid[...].reshape(tokens, m), TN).astype(BF16)
        for j in range(NY):
            w_send[g, j, 0:part] = got[j * part:(j + 1) * part]
            w_send[g, j, part:2 * part] = got[D + j * part:D + (j + 1) * part]
        for d in range(1, NY):
            w_copy(g, d).start()

    def e_copy(g, d):
        other, where = z_at(d)
        return remote(e_send.at[g, other], e_recv.at[g, d - 1], e_ss.at[g, d - 1], e_rs.at[g, d - 1], where)

    def stage5(g):
        whole = w_send[g, y].astype(F32)
        for d in range(1, NY):
            w_copy(g, d).wait_recv()
            whole += w_recv[g, d - 1].astype(F32)
        for zh in range(NZH):
            for zl in range(NZL):
                e_send[g, zh * NZL + zl] = whole[zh * part:(zh + 1) * part, zl * ROWS:(zl + 1) * ROWS].astype(BF16)
        for d in range(1, nz):
            e_copy(g, d).start()

    def f_copy(g):
        return remote(f_send.at[g], f_recv.at[y], f_ss.at[g], f_rs.at[y], final_target(g))

    def stays(g):
        return jnp.logical_and(on_diagonal, g == x)

    def stage6(g):
        whole = e_send[g, zz].astype(F32)
        for d in range(1, nz):
            e_copy(g, d).wait_recv()
            whole += e_recv[g, d - 1].astype(F32)

        @pl.when(stays(g))
        def _():
            f_recv[y] = whole

        @pl.when(jnp.logical_not(stays(g)))
        def _():
            f_send[g] = whole
            f_copy(g).start()

    stages = (stage0, stage1, stage1b, stage2, stage3, stage4, stage5, stage6)

    slots = GROUPS * tiles

    def step(t, nothing):
        @pl.when(t < slots)
        def _():
            g = t // tiles

            @pl.when(t % tiles == 0)
            def _():
                acc[g % 2] = jnp.zeros((2, HC + 1, L, 2 * D), F32)
                pair_kv_in(g).wait_recv()

            attend(t)

            @pl.when(jnp.logical_and(t % tiles == tiles - 1, g + 1 < GROUPS))
            def _():
                to_pair(g + 1)

            @pl.when(t + 2 < GROUPS)
            def _():
                send_kv(t + 2)

            @pl.when(t + 1 < GROUPS)
            def _():
                pass_on(t + 1)

        for (first, pace), stage in zip(WHEN, stages):
            since = t - first

            @pl.when(jnp.logical_and(since % pace == 0, jnp.logical_and(since >= 0, since < GROUPS * pace)))
            def _():
                stage(since // pace)

        return nothing

    lax.fori_loop(0, WHEN[-1][0] + (GROUPS - 1) * WHEN[-1][1] + 1, step, 0)

    for q in range(NY):
        here = jnp.logical_and(on_diagonal, q == y)

        @pl.when(jnp.logical_not(here))
        def _():
            remote(f_send.at[0], f_recv.at[q], f_ss.at[0], f_rs.at[q], final_source(q)).wait_recv()

    w_out[...] = jnp.transpose(f_recv[...].reshape(D, ROWS))

    for t in range(GROUPS * tiles):
        dq_copy(t).wait()
    for g in range(GROUPS):
        if g > 0:
            kv_sent(g)

            @pl.when(passes_last)
            def _():
                for k in last_by:
                    to_last(g, k).wait_send()

            @pl.when(passes_first)
            def _():
                for k in first_by:
                    to_first(g, k).wait_send()

        pair_kv(g).wait_send()
        pair_grads(g).wait_send()
        for k in range(1, HC + 1):
            by, holds, plain = relay_roles(g, k)

            @pl.when(jnp.logical_not(by))
            def _():
                back(g, HC - k).wait_send()

            if k >= 2 and g < GROUPS - 1:

                @pl.when(jnp.logical_and(by, z_lo == NZL - 1))
                def _():
                    relay_down(g, k).wait_send()

            if k < HC and g < GROUPS - 1:

                @pl.when(jnp.logical_and(by, z_lo == 0))
                def _():
                    relay_up(g, k).wait_send()

        for d in range(1, NX):
            spread(g, d).wait_send()
        pair_spread(g, c).wait_send()
        for d in range(1, NY):
            w_copy(g, d).wait_send()
        for d in range(1, nz):
            e_copy(g, d).wait_send()

        @pl.when(jnp.logical_not(stays(g)))
        def _():
            f_copy(g).wait_send()

    for dx in range(NX):
        for dc in range(2):
            for zl in range(NZL):
                if dx + dc:
                    hidden_copy(dx, dc, zl).wait_send()


def body(hidden, queries, keys, values, out_grad, positions):
    nb, nz, m, part = 2 * HC + 1, NZL * NZH, NZL * ROWS, D // NY
    tiles, lanes = SHARE // TILE, TILE * L
    vmem, dma = pltpu.VMEM, pltpu.SemaphoreType.DMA
    anywhere, inside = pl.BlockSpec(memory_space=pl.ANY), pl.BlockSpec(memory_space=pltpu.VMEM)
    pairs = GROUPS * SHARE * L * L * nb
    return pl.pallas_call(
        kernel,
        out_shape=(
            jax.ShapeDtypeStruct(queries.shape, BF16),
            jax.ShapeDtypeStruct((ROWS, D), F32),
        ),
        in_specs=[anywhere, anywhere, inside, inside, anywhere, inside],
        out_specs=(anywhere, inside),
        scratch_shapes=[
            vmem(queries.shape[1:], BF16),
            vmem(queries.shape[1:], BF16),
            vmem((GROUPS, HC + 1, 2, L, 2 * D), BF16),
            vmem((nb, L, L), F32),
            vmem((nb, L, lanes), F32),
            vmem((nb, L, lanes), F32),
            vmem((nb, L, lanes), BF16),
            vmem((nb, L, lanes), BF16),
            vmem((2, 2, HC + 1, L, 2 * D), F32),
            vmem((GROUPS * tiles, L, lanes), BF16),
            vmem((GROUPS, HC + 1, L, 2 * D), BF16),
            vmem((GROUPS, HC + 1, L, 2 * D), BF16),
            vmem((GROUPS, HC, L, 2 * D), BF16),
            vmem((GROUPS, HC, L, 2 * D), BF16),
            vmem((GROUPS, HC - 1, L, 2 * D), BF16),
            vmem((GROUPS, L, 2 * D), F32),
            vmem((GROUPS, NX, 2, L, 2 * D), BF16),
            vmem((NX * 2, L, m), BF16),
            vmem((GROUPS, NY, 2 * part, m), BF16),
            vmem((GROUPS, NY - 1, 2 * part, m), BF16),
            vmem((GROUPS, nz, part, ROWS), BF16),
            vmem((GROUPS, nz - 1, part, ROWS), BF16),
            vmem((GROUPS, part, ROWS), F32),
            vmem((NY, part, ROWS), F32),
            dma((2,)),
            dma((GROUPS * tiles,)),
            dma((GROUPS, HC)), dma((GROUPS, HC)), dma((GROUPS, HC)),
            dma((GROUPS,)), dma((GROUPS,)),
            dma((2 * NX, NZL)), dma((2 * NX, NZL)), dma((NZL,)),
            dma((GROUPS,)), dma((GROUPS,)),
            dma((GROUPS, HC)), dma((GROUPS, HC - 1)),
            dma((GROUPS, HC)), dma((GROUPS, HC)),
            dma((GROUPS, NX - 1)), dma((GROUPS, NX - 1)),
            dma((GROUPS,)), dma((GROUPS,)),
            dma((GROUPS, NY - 1)), dma((GROUPS, NY - 1)),
            dma((GROUPS, nz - 1)), dma((GROUPS, nz - 1)),
            dma((GROUPS,)), dma((NY,)),
        ],
        compiler_params=pltpu.CompilerParams(
            collective_id=0, has_side_effects=True, vmem_limit_bytes=56 * 2**20
        ),
        cost_estimate=pl.CostEstimate(
            flops=10 * pairs * D, bytes_accessed=12 * 2**20, transcendentals=pairs
        ),
    )(hidden, queries, keys, values, out_grad, positions)


def solution(mesh):
    rows = P("rep", "ctx", None)
    return jax.shard_map(
        body,
        mesh=mesh,
        in_specs=(rows, rows, rows, rows, rows, P("rep", "ctx")),
        out_specs=(rows, P("ctx", "rep")),
        check_vma=False,
    )
```

```python
import functools
import math

import jax
import jax.numpy as jnp
from jax import lax
from jax.experimental import pallas as pl
from jax.experimental.pallas import tpu as pltpu
from jax.sharding import PartitionSpec as P

GROUPS = 4
SHARE = 8
D = 128
L = 128
NY, NZL, NZH, NX = 4, 4, 2, 4
HC = 4
ROWS = 256
COPIES = 4
TILE = 4
WHEN = (
    (1, 3, 5, 7), (2, 4, 6, 8), (4, 6, 8, 8), (7, 8, 9, 10), (8, 9, 10, 11), (8, 9, 10, 11), (11, 11, 11, 12), (12, 12, 12, 13),
)

F32, BF16 = jnp.float32, jnp.bfloat16
NT = (((1,), (1,)), ((), ()))
TN = (((0,), (0,)), ((), ()))
NN = (((1,), (0,)), ((), ()))


def dot(a, b, dims):
    return lax.dot_general(a, b, dims, preferred_element_type=F32)


def kernel(
    hidden, queries, keys, values, out_grad, positions, dq_out, w_out,
    q_s, go_s, kv, bias, t_s, dp_s, w_s, ds_s, acc, dq_s,
    pair_send, pair_recv, back_send, back_recv, relay_recv, own_s, grads, hid, w_send, w_recv, e_send, e_recv, f_send, f_recv,
    in_sem, dq_sem, a_send, a_recv, fw_send, af_send, af_recv, h_send, h_recv, h_loc,
    p_ss, p_rs, r_ss, r_rs, b_ss, b_rs, g_ss, g_rs, gf_ss, gf_rs, w_ss, w_rs, e_ss, e_rs, f_ss, f_rs,
):
    nctx = NY * NZL * 2
    nz = NZL * NZH
    nb = 2 * HC + 1
    m = NZL * ROWS
    part = D // NY
    tiles = SHARE // TILE
    lanes = TILE * L
    scale = D ** -0.5

    i = lax.axis_index("ctx")
    r = lax.axis_index("rep")
    c = i % 2
    z_lo = (i // 2) % NZL
    y = i // (2 * NZL)
    x = r % NX
    z_hi = r // NX
    zz = z_hi * NZL + z_lo
    sib = i + 1 - 2 * c

    def at(ctx, rep):
        return {"ctx": ctx, "rep": rep}

    def ctx_of(yy, zl, cc):
        return (yy * NZL + zl) * 2 + cc

    def around(d):
        return (i + 2 * d + nctx) % nctx

    def rep_at(d):
        return z_hi * NX + (x + d) % NX

    def y_at(d):
        return (y + d) % NY

    def z_at(d):
        other = (zz + d) % nz
        return other, at(ctx_of(y, other % NZL, c), (other // NZL) * NX + x)

    q_in = pltpu.make_async_copy(queries.at[0], q_s, in_sem.at[0])
    go_in = pltpu.make_async_copy(out_grad.at[0], go_s, in_sem.at[1])
    q_in.start()
    go_in.start()

    barrier = pltpu.get_barrier_semaphore()
    partners = [at(sib, r)]
    for k in range(1, HC + 1):
        partners += [at(around(k), r), at(around(-k), r)]
    for d in range(1, NX):
        partners += [at(i, rep_at(d)), at(sib, rep_at(d))]
    for d in range(1, NY):
        partners.append(at(ctx_of(y_at(d), z_lo, c), r))
    for d in range(1, nz):
        partners.append(z_at(d)[1])
    for partner in partners:
        pl.semaphore_signal(barrier, inc=1, device_id=partner, device_id_type=pl.DeviceIdType.MESH)

    def final_target(g):
        return at(ctx_of(x, z_lo, c), z_hi * NX + g)

    def final_source(q):
        return at(ctx_of(q, z_lo, c), z_hi * NX + y)

    on_diagonal = x == y
    for g in range(NX):
        away = jnp.logical_not(jnp.logical_and(on_diagonal, g == x))

        @pl.when(away)
        def _():
            pl.semaphore_signal(barrier, inc=1, device_id=final_target(g), device_id_type=pl.DeviceIdType.MESH)
            pl.semaphore_signal(barrier, inc=1, device_id=final_source(g), device_id_type=pl.DeviceIdType.MESH)

    for g in range(GROUPS):
        kv[g, HC, c, :, 0:D] = keys[0, :, g * D:(g + 1) * D]
        kv[g, HC, c, :, D:2 * D] = values[0, :, g * D:(g + 1) * D]

    count = len(partners) + 2 * NX - 2 * jnp.where(on_diagonal, 1, 0)
    pl.semaphore_wait(barrier, count)

    def remote(src, dst, send, recv, where):
        return pltpu.make_async_remote_copy(
            src_ref=src, dst_ref=dst, send_sem=send, recv_sem=recv, device_id=where, device_id_type=pl.DeviceIdType.MESH
        )

    def halo(g, k):
        return remote(kv.at[g, HC, c], kv.at[g, HC - k, c], a_send.at[g, k - 1], a_recv.at[g, k - 1], at(around(k), r))

    def pair_kv(g):
        blocks = pl.ds(1 - c, HC)
        return remote(kv.at[g, blocks, c], kv.at[g, blocks, c], af_send.at[g], af_recv.at[g], at(sib, r))

    def pair_kv_in(g):
        blocks = pl.ds(c, HC)
        return remote(kv.at[g, blocks, 1 - c], kv.at[g, blocks, 1 - c], af_send.at[g], af_recv.at[g], at(sib, r))

    def direct(k):
        there = z_lo + k
        along = jnp.logical_and(there < NZL, jnp.logical_or(there < NZL - 1, k == 1))
        down = jnp.logical_and(there >= NZL, jnp.logical_or((there - NZL) % NZL > 0, k == HC))
        return jnp.logical_or(along, down)

    def to_last(g, k):
        there = at(around(1), r)
        return remote(kv.at[g, HC - k, c], kv.at[g, HC - k - 1, c], fw_send.at[g, k - 1], a_recv.at[g, k], there)

    def to_first(g, k):
        there = at(around(-1), r)
        return remote(kv.at[g, HC - k, c], kv.at[g, HC - k + 1, c], fw_send.at[g, k - 1], a_recv.at[g, k - 2], there)

    passes_last = jnp.logical_and(z_lo == NZL - 2, NZL > 2)
    passes_first = z_lo == 1
    last_by = range(1, NZL - 1)
    first_by = range(2, HC + 1)

    def send_kv(g):
        for k in range(1, HC + 1):

            @pl.when(jnp.logical_or(g == 0, direct(k)))
            def _():
                halo(g, k).start()

    def kv_sent(g):
        for k in range(1, HC + 1):

            @pl.when(jnp.logical_or(g == 0, direct(k)))
            def _():
                halo(g, k).wait_send()

    send_kv(0)

    def hidden_copy(dx, dc, zl):
        xx = (x + dx) % NX
        cc = (c + dc) % 2
        src = hidden.at[0, :, pl.ds(pl.multiple_of(((xx * NZL + zl) * 2 + cc) * ROWS, ROWS), ROWS)]
        dst = hid.at[2 * x + c, :, pl.ds(zl * ROWS, ROWS)]
        slot = 2 * dx + dc
        if slot == 0:
            return pltpu.make_async_copy(src, dst, h_loc.at[zl])
        return remote(src, dst, h_send.at[slot, zl], h_recv.at[slot, zl], at(ctx_of(y, z_lo, cc), rep_at(dx)))

    for dx in range(NX):
        for dc in range(2):
            for zl in range(NZL):
                hidden_copy(dx, dc, zl).start()

    token = lax.broadcasted_iota(jnp.int32, (L, L), 1) + i * L
    lowest = jnp.maximum(token - jnp.broadcast_to(positions[...], (L, L)), 0)
    for kc in range(nb):
        key = lax.broadcasted_iota(jnp.int32, (L, L), 0) + (i - 2 * HC + kc) * L
        seen = jnp.logical_and(key <= token, key >= lowest)
        bias[kc] = jnp.where(seen, 0.0, -1e30)

    q_in.wait()
    go_in.wait()


    def passes(k):
        return jnp.logical_or(
            jnp.logical_and(passes_last, k in last_by), jnp.logical_and(passes_first, k in first_by)
        )

    def pass_on(g):
        @pl.when(passes_last)
        def _():
            for k in last_by:
                halo(g, k).wait_recv()
                to_last(g, k).start()

        @pl.when(passes_first)
        def _():
            for k in reversed(first_by):
                halo(g, k).wait_recv()
                to_first(g, k).start()

    def to_pair(g):
        for k in range(1, HC + 1):

            @pl.when(jnp.logical_or(g == 0, jnp.logical_not(passes(k))))
            def _():
                halo(g, k).wait_recv()

        pair_kv(g).start()

    kv_sent(0)
    send_kv(1)
    to_pair(0)

    def attend(t):
        g = t // tiles
        cols = pl.ds(pl.multiple_of(t * lanes, lanes), lanes)
        q_wide = q_s[:, cols]
        go_wide = go_s[:, cols]
        q2 = jnp.concatenate([q_wide[:, j * D:(j + 1) * D] for j in range(TILE)], axis=0)
        go2 = jnp.concatenate([go_wide[:, j * D:(j + 1) * D] for j in range(TILE)], axis=0)

        def block(kc):
            b = c + kc
            return kv[g, b // 2, b % 2]

        def fold(v):
            return v.reshape(L // 8, 8, lanes)

        top = None
        for kc in range(nb):
            s = dot(block(kc)[:, 0:D], q2, NT) + jnp.concatenate([bias[kc]] * TILE, axis=1)
            t_s[kc] = s
            high = jnp.max(fold(s), axis=0)
            top = high if top is None else jnp.maximum(top, high)
        top = jnp.max(top, axis=0, keepdims=True)
        total = jnp.zeros((8, lanes), F32)
        delta = jnp.zeros((8, lanes), F32)
        for kc in range(nb):
            p = jnp.exp2((t_s[kc] - top) * (scale * math.log2(math.e)))
            dp = dot(block(kc)[:, D:2 * D], go2, NT)
            t_s[kc] = p
            dp_s[kc] = dp
            total += jnp.sum(fold(p), axis=0)
            delta += jnp.sum(fold(p * dp), axis=0)
        inverse = 1.0 / jnp.sum(total, axis=0, keepdims=True)
        delta = jnp.sum(delta, axis=0, keepdims=True) * inverse
        for kc in range(nb):
            p = t_s[kc] * inverse
            w_s[kc] = p.astype(BF16)
            ds_s[kc] = (p * (dp_s[kc] - delta)).astype(BF16)
        dq = jnp.zeros((lanes, D), F32)
        for kc in range(nb):
            b = c + kc
            ds = ds_s[kc]
            acc[g % 2, b % 2, b // 2, :, 0:D] += dot(ds, q2, NN)
            acc[g % 2, b % 2, b // 2, :, D:2 * D] += dot(w_s[kc], go2, NN)
            dq += dot(ds, block(kc)[:, 0:D], TN)
        dq = (dq * scale).astype(BF16)
        dq_s[t] = jnp.concatenate([dq[j * L:(j + 1) * L] for j in range(TILE)], axis=1)
        dq_copy(t).start()

    def dq_copy(t):
        cols = pl.ds(pl.multiple_of(t * lanes, lanes), lanes)
        return pltpu.make_async_copy(dq_s.at[t], dq_out.at[0, :, cols], dq_sem.at[t])

    def pair_grads(g):
        return remote(pair_send.at[g, pl.ds(c, HC)], pair_recv.at[g, pl.ds(c, HC)], p_ss.at[g], p_rs.at[g], at(sib, r))

    def pair_grads_in(g):
        blocks = pl.ds(1 - c, HC)
        return remote(pair_send.at[g, blocks], pair_recv.at[g, blocks], p_ss.at[g], p_rs.at[g], at(sib, r))

    def stage0(g):
        pair_send[g] = acc[g % 2, 1 - c].astype(BF16)
        pair_recv[g, HC * c] = jnp.zeros((L, 2 * D), BF16)
        pair_grads(g).start()

    def back(g, k):
        return remote(back_send.at[g, k], back_recv.at[g, k], b_ss.at[g, k], b_rs.at[g, k], at(around(k - HC), r))

    def comes_direct(k):
        along = jnp.logical_and(k <= z_lo, jnp.logical_or(z_lo < NZL - 1, k == 1))
        down = jnp.logical_and(k > z_lo, jnp.logical_or(z_lo > 0, k == HC))
        return jnp.logical_or(along, down)

    def relayed(g):
        return g < GROUPS - 1

    def relay_down(g, k):
        return remote(back_send.at[g, HC - k], relay_recv.at[g, k - 2], r_ss.at[g, k - 1], r_rs.at[g, k - 2], at(around(-1), r))

    def relay_up(g, k):
        return remote(back_send.at[g, HC - k], relay_recv.at[g, k - 1], r_ss.at[g, k - 1], r_rs.at[g, k - 1], at(around(1), r))

    def relay_roles(g, k):
        by = jnp.logical_and(relayed(g), jnp.logical_not(comes_direct(k)))
        holds = jnp.logical_and(relayed(g), passes(k))
        return by, holds, jnp.logical_not(jnp.logical_or(by, holds))

    def stage1(g):
        pair_grads_in(g).wait_recv()
        for k in range(1, HC + 1):
            n = HC - k
            back_send[g, n] = (acc[g % 2, c, n] + pair_recv[g, n].astype(F32)).astype(BF16)
            by, holds, plain = relay_roles(g, k)

            @pl.when(plain)
            def _():
                back(g, n).start()

            if k >= 2:

                @pl.when(jnp.logical_and(by, z_lo == NZL - 1))
                def _():
                    relay_down(g, k).start()

            if k < HC:

                @pl.when(jnp.logical_and(by, z_lo == 0))
                def _():
                    relay_up(g, k).start()

        own_s[g] = acc[g % 2, c, HC] + pair_recv[g, HC].astype(F32)

    def stage1b(g):
        def add_and_send(k, copy, slot):
            copy.wait_recv()
            n = HC - k
            back_send[g, n] = (back_send[g, n].astype(F32) + relay_recv[g, slot].astype(F32)).astype(BF16)
            back(g, n).start()

        @pl.when(jnp.logical_and(relayed(g), passes_last))
        def _():
            for k in last_by:
                add_and_send(k, relay_down(g, k + 1), k - 1)

        @pl.when(jnp.logical_and(relayed(g), passes_first))
        def _():
            for k in first_by:
                add_and_send(k, relay_up(g, k - 1), k - 2)

    def spread(g, d):
        mine = grads.at[g, x, c]
        return remote(mine, mine, g_ss.at[g, d - 1], g_rs.at[g, d - 1], at(i, rep_at(d)))

    def stage2(g):
        for k in range(1, HC + 1):

            @pl.when(jnp.logical_or(jnp.logical_not(relayed(g)), direct(k)))
            def _():
                back(g, HC - k).wait_recv()
                own_s[g] += back_recv[g, HC - k].astype(F32)

        whole = own_s[g]
        grads[g, x, c, :, 0:D] = (whole[:, 0:D] * scale).astype(BF16)
        grads[g, x, c, :, D:2 * D] = whole[:, D:2 * D].astype(BF16)
        for d in range(1, NX):
            spread(g, d).start()

    def pair_spread(g, cc):
        half = grads.at[g, :, cc]
        return remote(half, half, gf_ss.at[g], gf_rs.at[g], at(sib, r))

    def stage3(g):
        for d in range(1, NX):
            spread(g, d).wait_recv()
        pair_spread(g, c).start()

    def w_copy(g, d):
        return remote(w_send.at[g, y_at(d)], w_recv.at[g, d - 1], w_ss.at[g, d - 1], w_rs.at[g, d - 1],
                      at(ctx_of(y_at(d), z_lo, c), r))

    def stage4(g):
        @pl.when(g == 0)
        def _():
            for dx in range(NX):
                for dc in range(2):
                    for zl in range(NZL):
                        copy = hidden_copy(dx, dc, zl)
                        copy.wait() if dx + dc == 0 else copy.wait_recv()

        pair_spread(g, 1 - c).wait_recv()
        tokens = NX * 2 * L
        got = dot(grads[g].reshape(tokens, 2 * D), hid[...].reshape(tokens, m), TN).astype(BF16)
        for j in range(NY):
            w_send[g, j, 0:part] = got[j * part:(j + 1) * part]
            w_send[g, j, part:2 * part] = got[D + j * part:D + (j + 1) * part]
        for d in range(1, NY):
            w_copy(g, d).start()

    def e_copy(g, d):
        other, where = z_at(d)
        return remote(e_send.at[g, other], e_recv.at[g, d - 1], e_ss.at[g, d - 1], e_rs.at[g, d - 1], where)

    def stage5(g):
        whole = w_send[g, y].astype(F32)
        for d in range(1, NY):
            w_copy(g, d).wait_recv()
            whole += w_recv[g, d - 1].astype(F32)
        for zh in range(NZH):
            for zl in range(NZL):
                e_send[g, zh * NZL + zl] = whole[zh * part:(zh + 1) * part, zl * ROWS:(zl + 1) * ROWS].astype(BF16)
        for d in range(1, nz):
            e_copy(g, d).start()

    def f_copy(g):
        return remote(f_send.at[g], f_recv.at[y], f_ss.at[g], f_rs.at[y], final_target(g))

    def stays(g):
        return jnp.logical_and(on_diagonal, g == x)

    def stage6(g):
        whole = e_send[g, zz].astype(F32)
        for d in range(1, nz):
            e_copy(g, d).wait_recv()
            whole += e_recv[g, d - 1].astype(F32)

        @pl.when(stays(g))
        def _():
            f_recv[y] = whole

        @pl.when(jnp.logical_not(stays(g)))
        def _():
            f_send[g] = whole
            f_copy(g).start()

    stages = (stage0, stage1, stage1b, stage2, stage3, stage4, stage5, stage6)

    slots = GROUPS * tiles

    def step(t, nothing):
        @pl.when(t < slots)
        def _():
            g = t // tiles

            @pl.when(t % tiles == 0)
            def _():
                acc[g % 2] = jnp.zeros((2, HC + 1, L, 2 * D), F32)
                pair_kv_in(g).wait_recv()

            attend(t)

            @pl.when(jnp.logical_and(t % tiles == tiles - 1, g + 1 < GROUPS))
            def _():
                to_pair(g + 1)

            @pl.when(t + 2 < GROUPS)
            def _():
                send_kv(t + 2)

            @pl.when(t + 1 < GROUPS)
            def _():
                pass_on(t + 1)

        for when, stage in zip(WHEN, stages):
            begun = sum((t > slot).astype(jnp.int32) for slot in when[:GROUPS])
            due = sum((t >= slot).astype(jnp.int32) for slot in when[:GROUPS])

            def one(g, nothing, stage=stage):
                stage(g)
                return nothing

            lax.fori_loop(begun, due, one, 0)

        return nothing

    lax.fori_loop(0, WHEN[-1][-1] + 1, step, 0)

    for q in range(NY):
        here = jnp.logical_and(on_diagonal, q == y)

        @pl.when(jnp.logical_not(here))
        def _():
            remote(f_send.at[0], f_recv.at[q], f_ss.at[0], f_rs.at[q], final_source(q)).wait_recv()

    w_out[...] = jnp.transpose(f_recv[...].reshape(D, ROWS))

    for t in range(GROUPS * tiles):
        dq_copy(t).wait()
    for g in range(GROUPS):
        if g > 0:
            kv_sent(g)

            @pl.when(passes_last)
            def _():
                for k in last_by:
                    to_last(g, k).wait_send()

            @pl.when(passes_first)
            def _():
                for k in first_by:
                    to_first(g, k).wait_send()

        pair_kv(g).wait_send()
        pair_grads(g).wait_send()
        for k in range(1, HC + 1):
            by, holds, plain = relay_roles(g, k)

            @pl.when(jnp.logical_not(by))
            def _():
                back(g, HC - k).wait_send()

            if k >= 2 and g < GROUPS - 1:

                @pl.when(jnp.logical_and(by, z_lo == NZL - 1))
                def _():
                    relay_down(g, k).wait_send()

            if k < HC and g < GROUPS - 1:

                @pl.when(jnp.logical_and(by, z_lo == 0))
                def _():
                    relay_up(g, k).wait_send()

        for d in range(1, NX):
            spread(g, d).wait_send()
        pair_spread(g, c).wait_send()
        for d in range(1, NY):
            w_copy(g, d).wait_send()
        for d in range(1, nz):
            e_copy(g, d).wait_send()

        @pl.when(jnp.logical_not(stays(g)))
        def _():
            f_copy(g).wait_send()

    for dx in range(NX):
        for dc in range(2):
            for zl in range(NZL):
                if dx + dc:
                    hidden_copy(dx, dc, zl).wait_send()


def hand_over(dq, w, dq_out, w_out, dq_s, w_s, sem_in, sem_out):
    rows = L // COPIES
    parts = [(w, w_s, w_out)]
    for n in range(COPIES):
        part = pl.ds(n * rows, rows)
        parts.append((dq.at[0, part], dq_s.at[part], dq_out.at[0, part]))
    ins = [pltpu.make_async_copy(a, b, sem_in.at[n]) for n, (a, b, _) in enumerate(parts)]
    outs = [pltpu.make_async_copy(b, o, sem_out.at[n]) for n, (_, b, o) in enumerate(parts)]
    for copy in ins:
        copy.start()
    for arrived, copy in zip(ins, outs):
        arrived.wait()
        copy.start()
    for copy in outs:
        copy.wait()


def body(hidden, queries, keys, values, out_grad, positions):
    nb, nz, m, part = 2 * HC + 1, NZL * NZH, NZL * ROWS, D // NY
    tiles, lanes = SHARE // TILE, TILE * L
    vmem, dma = pltpu.VMEM, pltpu.SemaphoreType.DMA
    anywhere, inside = pl.BlockSpec(memory_space=pl.ANY), pl.BlockSpec(memory_space=pltpu.VMEM)
    pairs = GROUPS * SHARE * L * L * nb
    results = pl.pallas_call(
        kernel,
        out_shape=(
            jax.ShapeDtypeStruct(queries.shape, BF16),
            jax.ShapeDtypeStruct((ROWS, D), F32),
        ),
        in_specs=[anywhere, anywhere, inside, inside, anywhere, inside],
        out_specs=(anywhere, inside),
        scratch_shapes=[
            vmem(queries.shape[1:], BF16),
            vmem(queries.shape[1:], BF16),
            vmem((GROUPS, HC + 1, 2, L, 2 * D), BF16),
            vmem((nb, L, L), F32),
            vmem((nb, L, lanes), F32),
            vmem((nb, L, lanes), F32),
            vmem((nb, L, lanes), BF16),
            vmem((nb, L, lanes), BF16),
            vmem((2, 2, HC + 1, L, 2 * D), F32),
            vmem((GROUPS * tiles, L, lanes), BF16),
            vmem((GROUPS, HC + 1, L, 2 * D), BF16),
            vmem((GROUPS, HC + 1, L, 2 * D), BF16),
            vmem((GROUPS, HC, L, 2 * D), BF16),
            vmem((GROUPS, HC, L, 2 * D), BF16),
            vmem((GROUPS, HC - 1, L, 2 * D), BF16),
            vmem((GROUPS, L, 2 * D), F32),
            vmem((GROUPS, NX, 2, L, 2 * D), BF16),
            vmem((NX * 2, L, m), BF16),
            vmem((GROUPS, NY, 2 * part, m), BF16),
            vmem((GROUPS, NY - 1, 2 * part, m), BF16),
            vmem((GROUPS, nz, part, ROWS), BF16),
            vmem((GROUPS, nz - 1, part, ROWS), BF16),
            vmem((GROUPS, part, ROWS), F32),
            vmem((NY, part, ROWS), F32),
            dma((2,)),
            dma((GROUPS * tiles,)),
            dma((GROUPS, HC)), dma((GROUPS, HC)), dma((GROUPS, HC)),
            dma((GROUPS,)), dma((GROUPS,)),
            dma((2 * NX, NZL)), dma((2 * NX, NZL)), dma((NZL,)),
            dma((GROUPS,)), dma((GROUPS,)),
            dma((GROUPS, HC)), dma((GROUPS, HC - 1)),
            dma((GROUPS, HC)), dma((GROUPS, HC)),
            dma((GROUPS, NX - 1)), dma((GROUPS, NX - 1)),
            dma((GROUPS,)), dma((GROUPS,)),
            dma((GROUPS, NY - 1)), dma((GROUPS, NY - 1)),
            dma((GROUPS, nz - 1)), dma((GROUPS, nz - 1)),
            dma((GROUPS,)), dma((NY,)),
        ],
        compiler_params=pltpu.CompilerParams(
            collective_id=0, has_side_effects=True, vmem_limit_bytes=56 * 2**20
        ),
        cost_estimate=pl.CostEstimate(
            flops=10 * pairs * D, bytes_accessed=12 * 2**20, transcendentals=pairs
        ),
    )(hidden, queries, keys, values, out_grad, positions)
    return pl.pallas_call(
        hand_over,
        out_shape=tuple(jax.ShapeDtypeStruct(a.shape, a.dtype) for a in results),
        in_specs=[anywhere, anywhere],
        out_specs=(anywhere, anywhere),
        scratch_shapes=[vmem(queries.shape[1:], BF16), vmem((ROWS, D), F32), dma((COPIES + 1,)), dma((COPIES + 1,))],
    )(*results)


def solution(mesh):
    rows = P("rep", "ctx", None)
    return jax.shard_map(
        body,
        mesh=mesh,
        in_specs=(rows, rows, rows, rows, rows, P("rep", "ctx")),
        out_specs=(rows, P("ctx", "rep")),
        check_vma=False,
    )
```

```python
import functools
import math

import jax
import jax.numpy as jnp
from jax import lax
from jax.experimental import pallas as pl
from jax.experimental.pallas import tpu as pltpu
from jax.sharding import PartitionSpec as P

GROUPS = 4
SHARE = 8
D = 128
L = 128
NY, NZL, NZH, NX = 4, 4, 2, 4
HC = 4
ROWS = 256
COPIES = 4
TILE = 4
WHEN = (
    (1, 3, 5, 7), (2, 4, 6, 8), (4, 6, 8, 8), (7, 8, 9, 10), (8, 9, 10, 11), (8, 9, 10, 11), (11, 11, 12, 12), (12, 12, 13, 13),
)

F32, BF16 = jnp.float32, jnp.bfloat16
NT = (((1,), (1,)), ((), ()))
TN = (((0,), (0,)), ((), ()))
NN = (((1,), (0,)), ((), ()))


def dot(a, b, dims):
    return lax.dot_general(a, b, dims, preferred_element_type=F32)


def kernel(
    hidden, queries, keys, values, out_grad, positions, dq_out, w_out,
    q_s, go_s, kv, bias, t_s, dp_s, w_s, ds_s, acc, dq_s,
    pair_send, pair_recv, back_send, back_recv, relay_recv, own_s, grads, hid, w_send, w_recv, e_send, e_recv, f_send, f_recv,
    in_sem, dq_sem, a_send, a_recv, fw_send, af_send, af_recv, h_send, h_recv, h_loc,
    p_ss, p_rs, r_ss, r_rs, b_ss, b_rs, g_ss, g_rs, gf_ss, gf_rs, w_ss, w_rs, e_ss, e_rs, f_ss, f_rs,
):
    nctx = NY * NZL * 2
    nz = NZL * NZH
    nb = 2 * HC + 1
    m = NZL * ROWS
    part = D // NY
    tiles = SHARE // TILE
    lanes = TILE * L
    scale = D ** -0.5

    i = lax.axis_index("ctx")
    r = lax.axis_index("rep")
    c = i % 2
    z_lo = (i // 2) % NZL
    y = i // (2 * NZL)
    x = r % NX
    z_hi = r // NX
    zz = z_hi * NZL + z_lo
    sib = i + 1 - 2 * c

    def at(ctx, rep):
        return {"ctx": ctx, "rep": rep}

    def ctx_of(yy, zl, cc):
        return (yy * NZL + zl) * 2 + cc

    def around(d):
        return (i + 2 * d + nctx) % nctx

    def rep_at(d):
        return z_hi * NX + (x + d) % NX

    def y_at(d):
        return (y + d) % NY

    def z_at(d):
        other = (zz + d) % nz
        return other, at(ctx_of(y, other % NZL, c), (other // NZL) * NX + x)

    q_in = pltpu.make_async_copy(queries.at[0], q_s, in_sem.at[0])
    go_in = pltpu.make_async_copy(out_grad.at[0], go_s, in_sem.at[1])
    q_in.start()
    go_in.start()

    barrier = pltpu.get_barrier_semaphore()
    partners = [at(sib, r)]
    for k in range(1, HC + 1):
        partners += [at(around(k), r), at(around(-k), r)]
    for d in range(1, NX):
        partners += [at(i, rep_at(d)), at(sib, rep_at(d))]
    for d in range(1, NY):
        partners.append(at(ctx_of(y_at(d), z_lo, c), r))
    for d in range(1, nz):
        partners.append(z_at(d)[1])
    for partner in partners:
        pl.semaphore_signal(barrier, inc=1, device_id=partner, device_id_type=pl.DeviceIdType.MESH)

    def final_target(g):
        return at(ctx_of(x, z_lo, c), z_hi * NX + g)

    def final_source(q):
        return at(ctx_of(q, z_lo, c), z_hi * NX + y)

    on_diagonal = x == y
    for g in range(NX):
        away = jnp.logical_not(jnp.logical_and(on_diagonal, g == x))

        @pl.when(away)
        def _():
            pl.semaphore_signal(barrier, inc=1, device_id=final_target(g), device_id_type=pl.DeviceIdType.MESH)
            pl.semaphore_signal(barrier, inc=1, device_id=final_source(g), device_id_type=pl.DeviceIdType.MESH)

    for g in range(GROUPS):
        kv[g, HC, c, :, 0:D] = keys[0, :, g * D:(g + 1) * D]
        kv[g, HC, c, :, D:2 * D] = values[0, :, g * D:(g + 1) * D]

    count = len(partners) + 2 * NX - 2 * jnp.where(on_diagonal, 1, 0)
    pl.semaphore_wait(barrier, count)

    def remote(src, dst, send, recv, where):
        return pltpu.make_async_remote_copy(
            src_ref=src, dst_ref=dst, send_sem=send, recv_sem=recv, device_id=where, device_id_type=pl.DeviceIdType.MESH
        )

    def halo(g, k):
        return remote(kv.at[g, HC, c], kv.at[g, HC - k, c], a_send.at[g, k - 1], a_recv.at[g, k - 1], at(around(k), r))

    def pair_kv(g):
        blocks = pl.ds(1 - c, HC)
        return remote(kv.at[g, blocks, c], kv.at[g, blocks, c], af_send.at[g], af_recv.at[g], at(sib, r))

    def pair_kv_in(g):
        blocks = pl.ds(c, HC)
        return remote(kv.at[g, blocks, 1 - c], kv.at[g, blocks, 1 - c], af_send.at[g], af_recv.at[g], at(sib, r))

    def direct(k):
        there = z_lo + k
        along = jnp.logical_and(there < NZL, jnp.logical_or(there < NZL - 1, k == 1))
        down = jnp.logical_and(there >= NZL, jnp.logical_or((there - NZL) % NZL > 0, k == HC))
        return jnp.logical_or(along, down)

    def to_last(g, k):
        there = at(around(1), r)
        return remote(kv.at[g, HC - k, c], kv.at[g, HC - k - 1, c], fw_send.at[g, k - 1], a_recv.at[g, k], there)

    def to_first(g, k):
        there = at(around(-1), r)
        return remote(kv.at[g, HC - k, c], kv.at[g, HC - k + 1, c], fw_send.at[g, k - 1], a_recv.at[g, k - 2], there)

    passes_last = jnp.logical_and(z_lo == NZL - 2, NZL > 2)
    passes_first = z_lo == 1
    last_by = range(1, NZL - 1)
    first_by = range(2, HC + 1)

    def send_kv(g):
        for k in range(1, HC + 1):

            @pl.when(jnp.logical_or(g == 0, direct(k)))
            def _():
                halo(g, k).start()

    def kv_sent(g):
        for k in range(1, HC + 1):

            @pl.when(jnp.logical_or(g == 0, direct(k)))
            def _():
                halo(g, k).wait_send()

    send_kv(0)

    def hidden_copy(dx, dc, zl):
        xx = (x + dx) % NX
        cc = (c + dc) % 2
        src = hidden.at[0, :, pl.ds(pl.multiple_of(((xx * NZL + zl) * 2 + cc) * ROWS, ROWS), ROWS)]
        dst = hid.at[2 * x + c, :, pl.ds(zl * ROWS, ROWS)]
        slot = 2 * dx + dc
        if slot == 0:
            return pltpu.make_async_copy(src, dst, h_loc.at[zl])
        return remote(src, dst, h_send.at[slot, zl], h_recv.at[slot, zl], at(ctx_of(y, z_lo, cc), rep_at(dx)))

    for dx in range(NX):
        for dc in range(2):
            for zl in range(NZL):
                hidden_copy(dx, dc, zl).start()

    token = lax.broadcasted_iota(jnp.int32, (L, L), 1) + i * L
    lowest = jnp.maximum(token - jnp.broadcast_to(positions[...], (L, L)), 0)
    for kc in range(nb):
        key = lax.broadcasted_iota(jnp.int32, (L, L), 0) + (i - 2 * HC + kc) * L
        seen = jnp.logical_and(key <= token, key >= lowest)
        bias[kc] = jnp.where(seen, 0.0, -1e30)

    q_in.wait()
    go_in.wait()


    def passes(k):
        return jnp.logical_or(
            jnp.logical_and(passes_last, k in last_by), jnp.logical_and(passes_first, k in first_by)
        )

    def pass_on(g):
        @pl.when(passes_last)
        def _():
            for k in last_by:
                halo(g, k).wait_recv()
                to_last(g, k).start()

        @pl.when(passes_first)
        def _():
            for k in reversed(first_by):
                halo(g, k).wait_recv()
                to_first(g, k).start()

    def to_pair(g):
        for k in range(1, HC + 1):

            @pl.when(jnp.logical_or(g == 0, jnp.logical_not(passes(k))))
            def _():
                halo(g, k).wait_recv()

        pair_kv(g).start()

    kv_sent(0)
    send_kv(1)
    to_pair(0)

    def attend(t):
        g = t // tiles
        cols = pl.ds(pl.multiple_of(t * lanes, lanes), lanes)
        q_wide = q_s[:, cols]
        go_wide = go_s[:, cols]
        q2 = jnp.concatenate([q_wide[:, j * D:(j + 1) * D] for j in range(TILE)], axis=0)
        go2 = jnp.concatenate([go_wide[:, j * D:(j + 1) * D] for j in range(TILE)], axis=0)

        def block(kc):
            b = c + kc
            return kv[g, b // 2, b % 2]

        def fold(v):
            return v.reshape(L // 8, 8, lanes)

        top = None
        for kc in range(nb):
            s = dot(block(kc)[:, 0:D], q2, NT) + jnp.concatenate([bias[kc]] * TILE, axis=1)
            t_s[kc] = s
            high = jnp.max(fold(s), axis=0)
            top = high if top is None else jnp.maximum(top, high)
        top = jnp.max(top, axis=0, keepdims=True)
        total = jnp.zeros((8, lanes), F32)
        delta = jnp.zeros((8, lanes), F32)
        for kc in range(nb):
            p = jnp.exp2((t_s[kc] - top) * (scale * math.log2(math.e)))
            dp = dot(block(kc)[:, D:2 * D], go2, NT)
            t_s[kc] = p
            dp_s[kc] = dp
            total += jnp.sum(fold(p), axis=0)
            delta += jnp.sum(fold(p * dp), axis=0)
        inverse = 1.0 / jnp.sum(total, axis=0, keepdims=True)
        delta = jnp.sum(delta, axis=0, keepdims=True) * inverse
        for kc in range(nb):
            p = t_s[kc] * inverse
            w_s[kc] = p.astype(BF16)
            ds_s[kc] = (p * (dp_s[kc] - delta)).astype(BF16)
        dq = jnp.zeros((lanes, D), F32)
        for kc in range(nb):
            b = c + kc
            ds = ds_s[kc]
            acc[g % 2, b % 2, b // 2, :, 0:D] += dot(ds, q2, NN)
            acc[g % 2, b % 2, b // 2, :, D:2 * D] += dot(w_s[kc], go2, NN)
            dq += dot(ds, block(kc)[:, 0:D], TN)
        dq = (dq * scale).astype(BF16)
        dq_s[t] = jnp.concatenate([dq[j * L:(j + 1) * L] for j in range(TILE)], axis=1)
        dq_copy(t).start()

    def dq_copy(t):
        cols = pl.ds(pl.multiple_of(t * lanes, lanes), lanes)
        return pltpu.make_async_copy(dq_s.at[t], dq_out.at[0, :, cols], dq_sem.at[t])

    def pair_grads(g):
        return remote(pair_send.at[g, pl.ds(c, HC)], pair_recv.at[g, pl.ds(c, HC)], p_ss.at[g], p_rs.at[g], at(sib, r))

    def pair_grads_in(g):
        blocks = pl.ds(1 - c, HC)
        return remote(pair_send.at[g, blocks], pair_recv.at[g, blocks], p_ss.at[g], p_rs.at[g], at(sib, r))

    def stage0(g):
        pair_send[g] = acc[g % 2, 1 - c].astype(BF16)
        pair_recv[g, HC * c] = jnp.zeros((L, 2 * D), BF16)
        pair_grads(g).start()

    def back(g, k):
        return remote(back_send.at[g, k], back_recv.at[g, k], b_ss.at[g, k], b_rs.at[g, k], at(around(k - HC), r))

    def comes_direct(k):
        along = jnp.logical_and(k <= z_lo, jnp.logical_or(z_lo < NZL - 1, k == 1))
        down = jnp.logical_and(k > z_lo, jnp.logical_or(z_lo > 0, k == HC))
        return jnp.logical_or(along, down)

    def relayed(g):
        return jnp.logical_and(g >= 1, g < GROUPS - 1)

    def relay_down(g, k):
        return remote(back_send.at[g, HC - k], relay_recv.at[g, k - 2], r_ss.at[g, k - 1], r_rs.at[g, k - 2], at(around(-1), r))

    def relay_up(g, k):
        return remote(back_send.at[g, HC - k], relay_recv.at[g, k - 1], r_ss.at[g, k - 1], r_rs.at[g, k - 1], at(around(1), r))

    def relay_roles(g, k):
        by = jnp.logical_and(relayed(g), jnp.logical_not(comes_direct(k)))
        holds = jnp.logical_and(relayed(g), passes(k))
        return by, holds, jnp.logical_not(jnp.logical_or(by, holds))

    def stage1(g):
        pair_grads_in(g).wait_recv()
        for k in range(1, HC + 1):
            n = HC - k
            back_send[g, n] = (acc[g % 2, c, n] + pair_recv[g, n].astype(F32)).astype(BF16)
            by, holds, plain = relay_roles(g, k)

            @pl.when(plain)
            def _():
                back(g, n).start()

            if k >= 2:

                @pl.when(jnp.logical_and(by, z_lo == NZL - 1))
                def _():
                    relay_down(g, k).start()

            if k < HC:

                @pl.when(jnp.logical_and(by, z_lo == 0))
                def _():
                    relay_up(g, k).start()

        own_s[g] = acc[g % 2, c, HC] + pair_recv[g, HC].astype(F32)

    def stage1b(g):
        def add_and_send(k, copy, slot):
            copy.wait_recv()
            n = HC - k
            back_send[g, n] = (back_send[g, n].astype(F32) + relay_recv[g, slot].astype(F32)).astype(BF16)
            back(g, n).start()

        @pl.when(jnp.logical_and(relayed(g), passes_last))
        def _():
            for k in last_by:
                add_and_send(k, relay_down(g, k + 1), k - 1)

        @pl.when(jnp.logical_and(relayed(g), passes_first))
        def _():
            for k in first_by:
                add_and_send(k, relay_up(g, k - 1), k - 2)

    def spread(g, d):
        mine = grads.at[g, x, c]
        return remote(mine, mine, g_ss.at[g, d - 1], g_rs.at[g, d - 1], at(i, rep_at(d)))

    def stage2(g):
        for k in range(1, HC + 1):

            @pl.when(jnp.logical_or(jnp.logical_not(relayed(g)), direct(k)))
            def _():
                back(g, HC - k).wait_recv()
                own_s[g] += back_recv[g, HC - k].astype(F32)

        whole = own_s[g]
        grads[g, x, c, :, 0:D] = (whole[:, 0:D] * scale).astype(BF16)
        grads[g, x, c, :, D:2 * D] = whole[:, D:2 * D].astype(BF16)
        for d in range(1, NX):
            spread(g, d).start()

    def pair_spread(g, cc):
        half = grads.at[g, :, cc]
        return remote(half, half, gf_ss.at[g], gf_rs.at[g], at(sib, r))

    def stage3(g):
        for d in range(1, NX):
            spread(g, d).wait_recv()
        pair_spread(g, c).start()

    def w_copy(g, d):
        return remote(w_send.at[g, y_at(d)], w_recv.at[g, d - 1], w_ss.at[g, d - 1], w_rs.at[g, d - 1],
                      at(ctx_of(y_at(d), z_lo, c), r))

    def stage4(g):
        @pl.when(g == 0)
        def _():
            for dx in range(NX):
                for dc in range(2):
                    for zl in range(NZL):
                        copy = hidden_copy(dx, dc, zl)
                        copy.wait() if dx + dc == 0 else copy.wait_recv()

        pair_spread(g, 1 - c).wait_recv()
        tokens = NX * 2 * L
        got = dot(grads[g].reshape(tokens, 2 * D), hid[...].reshape(tokens, m), TN).astype(BF16)
        for j in range(NY):
            w_send[g, j, 0:part] = got[j * part:(j + 1) * part]
            w_send[g, j, part:2 * part] = got[D + j * part:D + (j + 1) * part]
        for d in range(1, NY):
            w_copy(g, d).start()

    def e_copy(g, d):
        other, where = z_at(d)
        return remote(e_send.at[g, other], e_recv.at[g, d - 1], e_ss.at[g, d - 1], e_rs.at[g, d - 1], where)

    def stage5(g):
        whole = w_send[g, y].astype(F32)
        for d in range(1, NY):
            w_copy(g, d).wait_recv()
            whole += w_recv[g, d - 1].astype(F32)
        for zh in range(NZH):
            for zl in range(NZL):
                e_send[g, zh * NZL + zl] = whole[zh * part:(zh + 1) * part, zl * ROWS:(zl + 1) * ROWS].astype(BF16)
        for d in range(1, nz):
            e_copy(g, d).start()

    def f_copy(g):
        return remote(f_send.at[g], f_recv.at[y], f_ss.at[g], f_rs.at[y], final_target(g))

    def stays(g):
        return jnp.logical_and(on_diagonal, g == x)

    def stage6(g):
        whole = e_send[g, zz].astype(F32)
        for d in range(1, nz):
            e_copy(g, d).wait_recv()
            whole += e_recv[g, d - 1].astype(F32)

        @pl.when(stays(g))
        def _():
            f_recv[y] = whole

        @pl.when(jnp.logical_not(stays(g)))
        def _():
            f_send[g] = whole
            f_copy(g).start()

    stages = (stage0, stage1, stage1b, stage2, stage3, stage4, stage5, stage6)

    slots = GROUPS * tiles

    def step(t, nothing):
        @pl.when(t < slots)
        def _():
            g = t // tiles

            @pl.when(t % tiles == 0)
            def _():
                acc[g % 2] = jnp.zeros((2, HC + 1, L, 2 * D), F32)
                pair_kv_in(g).wait_recv()

            attend(t)

            @pl.when(jnp.logical_and(t % tiles == tiles - 1, g + 1 < GROUPS))
            def _():
                to_pair(g + 1)

            @pl.when(t + 2 < GROUPS)
            def _():
                send_kv(t + 2)

            @pl.when(t + 1 < GROUPS)
            def _():
                pass_on(t + 1)

        for when, stage in zip(WHEN, stages):
            begun = sum((t > slot).astype(jnp.int32) for slot in when[:GROUPS])
            due = sum((t >= slot).astype(jnp.int32) for slot in when[:GROUPS])

            def one(g, nothing, stage=stage):
                stage(g)
                return nothing

            lax.fori_loop(begun, due, one, 0)

        return nothing

    lax.fori_loop(0, WHEN[-1][-1] + 1, step, 0)

    for q in range(NY):
        here = jnp.logical_and(on_diagonal, q == y)

        @pl.when(jnp.logical_not(here))
        def _():
            remote(f_send.at[0], f_recv.at[q], f_ss.at[0], f_rs.at[q], final_source(q)).wait_recv()

    w_out[...] = jnp.transpose(f_recv[...].reshape(D, ROWS))

    for t in range(GROUPS * tiles):
        dq_copy(t).wait()
    for g in range(GROUPS):
        if g > 0:
            kv_sent(g)

            @pl.when(passes_last)
            def _():
                for k in last_by:
                    to_last(g, k).wait_send()

            @pl.when(passes_first)
            def _():
                for k in first_by:
                    to_first(g, k).wait_send()

        pair_kv(g).wait_send()
        pair_grads(g).wait_send()
        for k in range(1, HC + 1):
            by, holds, plain = relay_roles(g, k)

            @pl.when(jnp.logical_not(by))
            def _():
                back(g, HC - k).wait_send()

            if k >= 2 and 1 <= g < GROUPS - 1:

                @pl.when(jnp.logical_and(by, z_lo == NZL - 1))
                def _():
                    relay_down(g, k).wait_send()

            if k < HC and 1 <= g < GROUPS - 1:

                @pl.when(jnp.logical_and(by, z_lo == 0))
                def _():
                    relay_up(g, k).wait_send()

        for d in range(1, NX):
            spread(g, d).wait_send()
        pair_spread(g, c).wait_send()
        for d in range(1, NY):
            w_copy(g, d).wait_send()
        for d in range(1, nz):
            e_copy(g, d).wait_send()

        @pl.when(jnp.logical_not(stays(g)))
        def _():
            f_copy(g).wait_send()

    for dx in range(NX):
        for dc in range(2):
            for zl in range(NZL):
                if dx + dc:
                    hidden_copy(dx, dc, zl).wait_send()


def hand_over(dq, w, dq_out, w_out, dq_s, w_s, sem_in, sem_out):
    rows = L // COPIES
    parts = [(w, w_s, w_out)]
    for n in range(COPIES):
        part = pl.ds(n * rows, rows)
        parts.append((dq.at[0, part], dq_s.at[part], dq_out.at[0, part]))
    ins = [pltpu.make_async_copy(a, b, sem_in.at[n]) for n, (a, b, _) in enumerate(parts)]
    outs = [pltpu.make_async_copy(b, o, sem_out.at[n]) for n, (_, b, o) in enumerate(parts)]
    for copy in ins:
        copy.start()
    for arrived, copy in zip(ins, outs):
        arrived.wait()
        copy.start()
    for copy in outs:
        copy.wait()


def body(hidden, queries, keys, values, out_grad, positions):
    nb, nz, m, part = 2 * HC + 1, NZL * NZH, NZL * ROWS, D // NY
    tiles, lanes = SHARE // TILE, TILE * L
    vmem, dma = pltpu.VMEM, pltpu.SemaphoreType.DMA
    anywhere, inside = pl.BlockSpec(memory_space=pl.ANY), pl.BlockSpec(memory_space=pltpu.VMEM)
    pairs = GROUPS * SHARE * L * L * nb
    results = pl.pallas_call(
        kernel,
        out_shape=(
            jax.ShapeDtypeStruct(queries.shape, BF16),
            jax.ShapeDtypeStruct((ROWS, D), F32),
        ),
        in_specs=[anywhere, anywhere, inside, inside, anywhere, inside],
        out_specs=(anywhere, inside),
        scratch_shapes=[
            vmem(queries.shape[1:], BF16),
            vmem(queries.shape[1:], BF16),
            vmem((GROUPS, HC + 1, 2, L, 2 * D), BF16),
            vmem((nb, L, L), F32),
            vmem((nb, L, lanes), F32),
            vmem((nb, L, lanes), F32),
            vmem((nb, L, lanes), BF16),
            vmem((nb, L, lanes), BF16),
            vmem((2, 2, HC + 1, L, 2 * D), F32),
            vmem((GROUPS * tiles, L, lanes), BF16),
            vmem((GROUPS, HC + 1, L, 2 * D), BF16),
            vmem((GROUPS, HC + 1, L, 2 * D), BF16),
            vmem((GROUPS, HC, L, 2 * D), BF16),
            vmem((GROUPS, HC, L, 2 * D), BF16),
            vmem((GROUPS, HC - 1, L, 2 * D), BF16),
            vmem((GROUPS, L, 2 * D), F32),
            vmem((GROUPS, NX, 2, L, 2 * D), BF16),
            vmem((NX * 2, L, m), BF16),
            vmem((GROUPS, NY, 2 * part, m), BF16),
            vmem((GROUPS, NY - 1, 2 * part, m), BF16),
            vmem((GROUPS, nz, part, ROWS), BF16),
            vmem((GROUPS, nz - 1, part, ROWS), BF16),
            vmem((GROUPS, part, ROWS), F32),
            vmem((NY, part, ROWS), F32),
            dma((2,)),
            dma((GROUPS * tiles,)),
            dma((GROUPS, HC)), dma((GROUPS, HC)), dma((GROUPS, HC)),
            dma((GROUPS,)), dma((GROUPS,)),
            dma((2 * NX, NZL)), dma((2 * NX, NZL)), dma((NZL,)),
            dma((GROUPS,)), dma((GROUPS,)),
            dma((GROUPS, HC)), dma((GROUPS, HC - 1)),
            dma((GROUPS, HC)), dma((GROUPS, HC)),
            dma((GROUPS, NX - 1)), dma((GROUPS, NX - 1)),
            dma((GROUPS,)), dma((GROUPS,)),
            dma((GROUPS, NY - 1)), dma((GROUPS, NY - 1)),
            dma((GROUPS, nz - 1)), dma((GROUPS, nz - 1)),
            dma((GROUPS,)), dma((NY,)),
        ],
        compiler_params=pltpu.CompilerParams(
            collective_id=0, has_side_effects=True, vmem_limit_bytes=56 * 2**20
        ),
        cost_estimate=pl.CostEstimate(
            flops=10 * pairs * D, bytes_accessed=12 * 2**20, transcendentals=pairs
        ),
    )(hidden, queries, keys, values, out_grad, positions)
    return pl.pallas_call(
        hand_over,
        out_shape=tuple(jax.ShapeDtypeStruct(a.shape, a.dtype) for a in results),
        in_specs=[anywhere, anywhere],
        out_specs=(anywhere, anywhere),
        scratch_shapes=[vmem(queries.shape[1:], BF16), vmem((ROWS, D), F32), dma((COPIES + 1,)), dma((COPIES + 1,))],
    )(*results)


def solution(mesh):
    rows = P("rep", "ctx", None)
    return jax.shard_map(
        body,
        mesh=mesh,
        in_specs=(rows, rows, rows, rows, rows, P("rep", "ctx")),
        out_specs=(rows, P("ctx", "rep")),
        check_vma=False,
    )
```
